32 devices in a mesh: dp: 8 (over z, x), fsdp: 4 (over y, core).
Axes of the slice: x: 2, y: 2, z: 4, core: 2. Of those that a mesh axis runs over, the one named last changes fastest.
Arguments:
- inputs: bfloat16 [32, 384, 768], P(('dp', 'fsdp')), may hold values from -6 to 6
- groups: int32 [32, 384], P(('dp', 'fsdp')), may hold values from 0 to 5, never falling along the last dimension, each value on 1 to 192 neighbouring positions
- padding: int32 [32], P(('dp', 'fsdp')), may hold values from 0 to 191
- cotangent: bfloat16 [32, 384, 768], P(('dp', 'fsdp')), may hold values from -6 to 6
- attn_gain: bfloat16 [2, 768], P(None, 'fsdp'), may hold values from 0.5 to 1.5
- attn_shift: bfloat16 [2, 768], P(None, 'fsdp'), may hold values from -2 to 2
- qkv_weight: bfloat16 [2, 768, 2304], P(None, 'fsdp'), may hold values from -0.21875 to 0.21875
- query_bias: bfloat16 [2, 768], P(None, 'fsdp'), may hold values from -2 to 2
- value_bias: bfloat16 [2, 768], P(None, 'fsdp'), may hold values from -2 to 2
- out_weight: bfloat16 [2, 768, 768], P(None, 'fsdp'), may hold values from -0.875 to 0.875
- out_bias: bfloat16 [2, 768], P(None, 'fsdp'), may hold values from -2 to 2
- mlp_gain: bfloat16 [2, 768], P(None, 'fsdp'), may hold values from 0.5 to 1.5
- mlp_shift: bfloat16 [2, 768], P(None, 'fsdp'), may hold values from -2 to 2
- fc_weight: bfloat16 [2, 768, 3072], P(None, 'fsdp'), may hold values from -0.21875 to 0.21875
- fc_bias: bfloat16 [2, 3072], P(None, 'fsdp'), may hold values from -2 to 2
- proj_weight: bfloat16 [2, 3072, 768], P(None, 'fsdp'), may hold values from -0.15625 to 0.15625
- proj_bias: bfloat16 [2, 768], P(None, 'fsdp'), may hold values from -2 to 2
Outputs:
- layer_out: bfloat16 [32, 384, 768], P(('dp', 'fsdp'))
- input_grad: float32 [32, 384, 768], P(('dp', 'fsdp'))
- attn_gain_grad: float32 [2, 768], P(None, 'fsdp')
- attn_shift_grad: float32 [2, 768], P(None, 'fsdp')
- qkv_weight_grad: float32 [2, 768, 2304], P(None, 'fsdp')
- query_bias_grad: float32 [2, 768], P(None, 'fsdp')
- value_bias_grad: float32 [2, 768], P(None, 'fsdp')
- out_weight_grad: float32 [2, 768, 768], P(None, 'fsdp')
- out_bias_grad: float32 [2, 768], P(None, 'fsdp')
- mlp_gain_grad: float32 [2, 768], P(None, 'fsdp')
- mlp_shift_grad: float32 [2, 768], P(None, 'fsdp')
- fc_weight_grad: float32 [2, 768, 3072], P(None, 'fsdp')
- fc_bias_grad: float32 [2, 3072], P(None, 'fsdp')
- proj_weight_grad: float32 [2, 3072, 768], P(None, 'fsdp')
- proj_bias_grad: float32 [2, 768], P(None, 'fsdp')
The draws below stay inside these ranges and needn't reach their ends.
Inputs may be any that keep to these rules, and one draw needn't show every extreme that they name: `groups`: group numbers never fall along a sequence; each group holds 1 to 192 positions, and one holds exactly that many.
All inputs are finite; a program needn't handle non-finite values.
Results may differ from the reference program's by a relative error of at most 0.02.
Values may be sent and summed in bfloat16 or wider, within the bound.
No kernel may reach another device: no remote copies, remote signals or barrier semaphores. Data moves between devices by JAX's collectives and lax.ppermute only.
A program may use at most 256 MiB of HBM per device.

```python
import math
import jax
import jax.numpy as jnp
import numpy as np
from jax import lax

D = 768
HEADS = 12
HEAD = 64
FF = 3072
LAYERS = 2
SEQ_LEN = 384
GROUPS = 6
SEQS = 32


def draw_padding(key, part):
    key = jax.random.fold_in(key, 11)
    first_key, second_key, third_key = jax.random.split(key, 3)
    values = jax.random.randint(first_key, (SEQS,), 0, SEQ_LEN // 2)
    chosen = jax.random.randint(second_key, (), 0, SEQS)
    offset = jax.random.randint(third_key, (), 1, SEQS)
    places = jnp.arange(SEQS, dtype=jnp.int32)
    values = jnp.where(places == chosen, SEQ_LEN // 2 - 1, values)
    values = jnp.where(places == (chosen + offset) % SEQS, 0, values)
    return values.astype(jnp.int32)


def steps_of(rng, dims, cuts, least, top_value):
    loudness = 1.0
    for dim, parts in cuts:
        steps = jax.random.uniform(jax.random.fold_in(jax.random.fold_in(rng, 6), dim), (parts,), jnp.float32, least / len(cuts), top_value / len(cuts))
        loudness = loudness * jnp.repeat(jnp.exp(steps), dims[dim] // parts).reshape((-1,) + (1,) * (len(dims) - 1 - dim))
    return loudness


def split_up(count, total, reach, lean):
    loads = [(1 << 20) // math.isqrt(rank ** lean) + 1 for rank in range(2, count + 1)]
    spare, counts = total - reach - (count - 1), [1] * (count - 1)
    while spare > 0:
        candidates = [i for i in range(count - 1) if counts[i] < reach]
        whole, remaining = sum([loads[i] for i in candidates]), spare
        for i in candidates:
            extra = min(reach - counts[i], max(1, remaining * loads[i] // whole), spare)
            counts[i] = counts[i] + extra
            spare = spare - extra
    return np.array([reach] + counts)


def ragged(key, amount, total, reach, slope):
    if amount == 2:
        one = jax.random.randint(key, (), max(1, total - reach), min(reach, total - 1) + 1)
        return jnp.stack([one, total - one])
    lengths = jnp.asarray(split_up(amount, total, reach, slope), jnp.int32)
    couples = (amount - 1) // 2
    donor, receiver = lengths[1:1 + 2 * couples:2], lengths[2:2 + 2 * couples:2]
    room = jnp.minimum(donor - 1, reach - receiver)
    shifted = jax.random.randint(jax.random.fold_in(key, 1), (couples,), 0, 1 << 20) % (room + 1)
    lengths = lengths.at[1:1 + 2 * couples:2].set(donor - shifted).at[2:2 + 2 * couples:2].set(receiver + shifted)
    return lengths[jax.random.permutation(jax.random.fold_in(key, 2), amount)]


def noise(own_key, dims, scale, bound, shards=(), held_as=jnp.bfloat16):
    values = scale * jax.random.normal(own_key, dims, jnp.float32)
    if shards:
        values = values * steps_of(own_key, dims, shards, -0.22, 0.18)
    return jnp.clip(values, -bound, bound).astype(held_as)


def setup_inputs(seed: int = 0) -> dict:
    arg_keys = jax.random.split(jax.random.key(seed), 18)
    inputs = noise(arg_keys[0], (SEQS, SEQ_LEN, D), 1.0, 6.0, ((0, 32),))
    groups = jax.vmap(lambda own: jnp.searchsorted(jnp.cumsum(ragged(own, GROUPS, SEQ_LEN, SEQ_LEN // 2, 2)), jnp.arange(SEQ_LEN), side="right"))(jax.random.split(arg_keys[1], SEQS)).reshape((SEQS, SEQ_LEN)).astype(jnp.int32)
    padding = draw_padding(jax.random.fold_in(arg_keys[17], 71), 0)
    cotangent = noise(arg_keys[3], (SEQS, SEQ_LEN, D), 1.0, 6.0, ((0, 32),))
    attn_gain = jnp.clip(1.0 + 0.1 * jax.random.normal(arg_keys[4], (LAYERS, D), jnp.float32), 0.5, 1.5).astype(jnp.bfloat16)
    attn_shift = noise(arg_keys[5], (LAYERS, D), 0.3, 2.0, ((1, 4),))
    qkv_weight = noise(arg_keys[6], (LAYERS, D, 3 * D), D ** -0.5, 0.21875, ((1, 4),))
    query_bias = noise(arg_keys[7], (LAYERS, D), 0.3, 2.0, ((1, 4),))
    value_bias = noise(arg_keys[8], (LAYERS, D), 0.3, 2.0, ((1, 4),))
    out_weight = noise(arg_keys[9], (LAYERS, D, D), (D // 16) ** -0.5, 0.875, ((1, 4),))
    out_bias = noise(arg_keys[10], (LAYERS, D), 0.3, 2.0, ((1, 4),))
    mlp_gain = jnp.clip(1.0 + 0.1 * jax.random.normal(arg_keys[11], (LAYERS, D), jnp.float32), 0.5, 1.5).astype(jnp.bfloat16)
    mlp_shift = noise(arg_keys[12], (LAYERS, D), 0.3, 2.0, ((1, 4),))
    fc_weight = noise(arg_keys[13], (LAYERS, D, FF), D ** -0.5, 0.21875, ((1, 4),))
    fc_bias = noise(arg_keys[14], (LAYERS, FF), 0.3, 2.0, ((1, 4),))
    proj_weight = noise(arg_keys[15], (LAYERS, FF, D), (FF // 2) ** -0.5, 0.15625, ((1, 4),))
    proj_bias = noise(arg_keys[16], (LAYERS, D), 0.3, 2.0, ((1, 4),))
    return {"inputs": inputs, "groups": groups, "padding": padding, "cotangent": cotangent, "attn_gain": attn_gain, "attn_shift": attn_shift, "qkv_weight": qkv_weight, "query_bias": query_bias, "value_bias": value_bias, "out_weight": out_weight, "out_bias": out_bias, "mlp_gain": mlp_gain, "mlp_shift": mlp_shift, "fc_weight": fc_weight, "fc_bias": fc_bias, "proj_weight": proj_weight, "proj_bias": proj_bias}


epsilon = 1e-05
highest = lax.Precision.HIGHEST

@jax.custom_vjp
def low(v):
    return lax.optimization_barrier(v.astype(jnp.bfloat16)).astype(jnp.float32)

@jax.custom_vjp
def low_back(v):
    return v

def low_keep(v):
    return (low(v), None)

def low_pass(kept, grad):
    return (grad,)

def back_keep(v):
    return (v, None)

def back_low(kept, grad):
    return (low(grad),)
low.defvjp(low_keep, low_pass)
low_back.defvjp(back_keep, back_low)

def layer_norm(hidden, gain_row, shift_row):
    average = lax.optimization_barrier(jnp.mean(hidden, axis=-1, keepdims=True))
    centred = hidden - average
    spread = lax.optimization_barrier(jnp.mean(centred * centred, axis=-1, keepdims=True))
    return centred * lax.rsqrt(spread + epsilon) * gain_row + shift_row

def attend_mask(groups, padding):
    length = groups.shape[-1]
    places = jnp.arange(length, dtype=jnp.int32)
    unpadded = places[None, :] < (length - padding)[:, None]
    causal = places[:, None] >= places[None, :]
    same_group = groups[:, :, None] == groups[:, None, :]
    allowed = same_group & causal[None] & unpadded[:, None, :]
    return allowed | (places[:, None] == places[None, :])[None]

def gpt_block(hidden, weights, allowed):
    attn_gain, attn_shift, qkv_weight, query_bias, value_bias, out_weight, out_bias, mlp_gain, mlp_shift, fc_weight, fc_bias, proj_weight, proj_bias = weights
    seqs_here, length, model_width = hidden.shape
    flat_rows = hidden.reshape(-1, model_width)
    normed = low(layer_norm(flat_rows, attn_gain, attn_shift))
    bias_row = jnp.concatenate([query_bias, jnp.zeros_like(query_bias), value_bias])
    packed = low(low_back(jnp.dot(normed, qkv_weight, precision=highest) + bias_row))
    columns = packed.reshape(seqs_here, length, 3, HEADS, HEAD)
    factor = HEAD ** (-0.5)
    scores = low_back(jnp.einsum('sqhd,skhd->shqk', columns[:, :, 0], columns[:, :, 1], precision=highest) * factor)
    scores = jnp.where(allowed[:, None], scores, -1e+30)
    biggest = lax.optimization_barrier(jnp.max(scores, axis=-1, keepdims=True))
    expo_s = jnp.exp(scores - biggest)
    softmax_w = expo_s / lax.optimization_barrier(jnp.sum(expo_s, axis=-1, keepdims=True))
    context = jnp.einsum('shqk,skhd->sqhd', low(softmax_w), columns[:, :, 2], precision=highest)
    context = low(low_back(context.reshape(-1, model_width)))
    after_attn = flat_rows + low_back(jnp.dot(context, out_weight, precision=highest) + out_bias)
    normed_two = low(layer_norm(after_attn, mlp_gain, mlp_shift))
    pre_act = low_back(jnp.dot(normed_two, fc_weight, precision=highest) + fc_bias)
    active = low(jax.nn.gelu(pre_act, approximate=True))
    result = after_attn + low_back(jnp.dot(active, proj_weight, precision=highest) + proj_bias)
    return result.reshape(seqs_here, length, model_width)

def forward_all(start_rows, params, allowed):
    hidden = start_rows
    for depth in range(LAYERS):
        hidden = gpt_block(hidden, tuple((member[depth] for member in params)), allowed)
    return hidden

def reference(inputs, groups, padding, cotangent, attn_gain, attn_shift, qkv_weight, query_bias, value_bias, out_weight, out_bias, mlp_gain, mlp_shift, fc_weight, fc_bias, proj_weight, proj_bias):
    params = tuple((member.astype(jnp.float32) for member in (attn_gain, attn_shift, qkv_weight, query_bias, value_bias, out_weight, out_bias, mlp_gain, mlp_shift, fc_weight, fc_bias, proj_weight, proj_bias)))
    bunch = 4
    count_b = SEQS // bunch
    stacked = (inputs.astype(jnp.float32).reshape(count_b, bunch, SEQ_LEN, D), groups.reshape(count_b, bunch, SEQ_LEN), padding.reshape(count_b, bunch), cotangent.astype(jnp.float32).reshape(count_b, bunch, SEQ_LEN, D))

    def step_fn(totals, item):
        inputs_b, groups_b, padding_b, cotan_b = item
        allowed = attend_mask(groups_b, padding_b)
        result, back_fn = jax.vjp(lambda start, weights_p: forward_all(start, weights_p, allowed), inputs_b, params)
        input_g, weight_g = back_fn(cotan_b)
        totals = jax.tree.map(lambda first, second: first + second, totals, weight_g)
        return (totals, (result, input_g))
    zeros_p = tuple((jnp.zeros_like(member) for member in params))
    totals, (results, input_grads) = lax.scan(step_fn, zeros_p, stacked)
    return (results.reshape(SEQS, SEQ_LEN, D).astype(jnp.bfloat16), input_grads.reshape(SEQS, SEQ_LEN, D), totals[0], totals[1], totals[2], totals[3], totals[4], totals[5], totals[6], totals[7], totals[8], totals[9], totals[10], totals[11], totals[12])
```

```python
import jax
import jax.numpy as jnp
from jax import lax
from jax.experimental import pallas as pl
from jax.experimental.pallas import tpu as pltpu
from jax.sharding import PartitionSpec as P

HEADS = 12
EPS = 1e-05
BIG = -1e30
VMEM_LIMIT = 56 * 1024 * 1024
F32 = jnp.float32
BF16 = jnp.bfloat16
VM = pl.BlockSpec(memory_space=pltpu.VMEM)
HB = pl.BlockSpec(memory_space=pl.ANY)


def swap(value, axis, bit, count):
    return lax.ppermute(value, axis, [(i, i ^ (1 << bit)) for i in range(count)])


def bits_of(count):
    bits = count.bit_length() - 1
    assert 1 << bits == count
    return bits


def take_half(value, which, dim):
    half = value.shape[dim] // 2
    return lax.dynamic_slice_in_dim(value, which * half, half, dim)


def put_halves(mine, other, which, dim):
    half = mine.shape[dim]
    shape = list(mine.shape)
    shape[dim] = 2 * half
    whole = jnp.zeros(shape, mine.dtype)
    whole = lax.dynamic_update_slice_in_dim(whole, mine, which * half, dim)
    return lax.dynamic_update_slice_in_dim(whole, other, (1 - which) * half, dim)


def add(first, second):
    return (first.astype(F32) + second.astype(F32)).astype(BF16)


def gather_pieces(shard, nf, nd):
    top = bits_of(nf) - 1
    helper = lax.axis_index("dp") & 1
    first = swap(take_half(shard, helper, 0), "fsdp", top, nf)
    second = swap(first, "dp", 0, nd)
    held = [(0, None, shard), (1 << top, 0, first), (1 << top, 1, second)]
    for bit in range(top):
        held += [(r | (1 << bit), part, swap(v, "fsdp", bit, nf)) for r, part, v in held]
    return held


def fetch(held, sources, place_ref, start, target, sem):
    nf = 1 + max(r for r, _, _ in held)
    rows, width = target.shape[0] // nf, target.shape[1]
    copies = []
    for (r, part, _), source in zip(held, sources):
        count = source.shape[0]
        offset = 0 if part is None else (place_ref[1] if part == 0 else 1 - place_ref[1]) * count
        first = pl.multiple_of((place_ref[0] ^ r) * rows + offset, 32)
        copies.append(
            pltpu.make_async_copy(
                source.at[:, pl.ds(start, width)], target.at[pl.ds(first, count), :], sem
            )
        )
    return copies


def start_all(copies):
    for copy in copies:
        copy.start()


def wait_all(copies):
    for copy in copies:
        copy.wait()


def nn(a, b):
    return jnp.dot(a, b, preferred_element_type=F32)


def nt(a, b):
    return lax.dot_general(a, b, (((1,), (1,)), ((), ())), preferred_element_type=F32)


def norm_parts(h):
    mean = jnp.mean(h, axis=-1, keepdims=True)
    centred = h - mean
    rstd = lax.rsqrt(jnp.mean(centred * centred, axis=-1, keepdims=True) + EPS)
    return centred * rstd, rstd


def flip(value):
    return value.astype(F32).T.astype(BF16)


def block(i, size):
    return pl.ds(pl.multiple_of(i * size, size), size)


def fill_bias(bias_ref, group_col, group_row, valid):
    length = group_col.shape[0]
    for qb in range(length // 128):
        keys = lax.broadcasted_iota(jnp.int32, (length, 128), 0)
        queries = lax.broadcasted_iota(jnp.int32, (length, 128), 1) + qb * 128
        same = group_col[...] == group_row[:, qb * 128 : (qb + 1) * 128]
        ok = (same & (keys <= queries) & (keys < valid)) | (keys == queries)
        tile = jnp.where(ok, 0.0, BIG).astype(F32)
        bias_ref[qb, :, 0:128] = tile
        bias_ref[qb, :, 128:256] = tile


def two_heads(rows):
    lane = lax.broadcasted_iota(jnp.int32, rows.shape, 1)
    zero = jnp.zeros_like(rows)
    return jnp.concatenate([jnp.where(lane < 64, rows, zero), jnp.where(lane < 64, zero, rows)], axis=0)


def own_heads(tile):
    return jnp.concatenate([tile[0:64, 0:128], tile[64:128, 128:256]], axis=0)


def call(body, place, args, weights, after, out_shape, scratch, micros):
    sources = [v for held, _, _ in weights for _, _, v in held]
    n_args, n_out, n_w = len(args), len(out_shape), len(weights)

    def kernel(place_ref, *refs):
        ins = refs[:n_args]
        src = refs[n_args : n_args + len(sources)]
        refs = refs[n_args + len(sources) + len(after) :]
        outs, tiles, sems = refs[:n_out], refs[n_out : n_out + n_w], refs[n_out + n_w : n_out + 2 * n_w]
        copies = []
        for (held, start, _), tile, sem in zip(weights, tiles, sems):
            copies.append(fetch(held, src[: len(held)], place_ref, start, tile, sem))
            src = src[len(held) :]
            start_all(copies[-1])
        waits = [lambda c=c: wait_all(c) for c in copies]
        body(place_ref, *ins, *outs, *tiles, *refs[n_out + 2 * n_w :], waits)

    return pl.pallas_call(
        kernel,
        grid_spec=pltpu.PrefetchScalarGridSpec(
            num_scalar_prefetch=1,
            grid=(),
            in_specs=[VM] * n_args + [HB] * (len(sources) + len(after)),
            out_specs=[VM] * n_out,
            scratch_shapes=[pltpu.VMEM(shape, BF16) for _, _, shape in weights]
            + [pltpu.SemaphoreType.DMA] * n_w + scratch,
        ),
        out_shape=[jax.ShapeDtypeStruct(s, d) for s, d in out_shape],
        compiler_params=pltpu.CompilerParams(vmem_limit_bytes=VMEM_LIMIT),
        cost_estimate=pl.CostEstimate(
            flops=int(micros * 1.15e9), bytes_accessed=8 << 20, transcendentals=0
        ),
    )(place, *args, *sources, *after)


def attn_forward(place, weights, after, hidden, gain, shift, qkv_bias, out_bias, group_col, group_row):
    length, width = hidden.shape
    qkv_width = qkv_bias.shape[1]
    pairs = width // 128
    blocks = length // 128

    def body(place_ref, h_ref, g_ref, b_ref, qb_ref, ob_ref, gc_ref, gr_ref,
             qkv_ref, ctx_t_ref, lse_ref, out_ref, wq_ref, wo_ref, a_ref, bias_ref, ctx_ref, waits):
        xhat, _ = norm_parts(h_ref[...].astype(F32))
        a_ref[...] = (xhat * g_ref[...] + b_ref[...]).astype(BF16)
        fill_bias(bias_ref, gc_ref, gr_ref, place_ref[2])
        waits[0]()

        @pl.loop(0, qkv_width // 256)
        def _(i):
            cols = block(i, 256)
            qkv_ref[:, cols] = (nn(a_ref[...], wq_ref[:, cols]) + qb_ref[:, cols]).astype(BF16)

        @pl.loop(0, pairs)
        def _(hp):
            q2 = qkv_ref[:, block(hp, 128)] * jnp.asarray(0.125, BF16)
            k2 = qkv_ref[:, block(hp + pairs, 128)]
            v2t = flip(qkv_ref[:, block(hp + 2 * pairs, 128)])
            for qb in range(blocks):
                nk = (qb + 1) * 128
                s = nt(k2[:nk], two_heads(q2[qb * 128 : nk])) + bias_ref[qb, 0:nk, :]
                top = jnp.max(s, axis=0, keepdims=True)
                p = jnp.exp(s - top)
                total = jnp.sum(p, axis=0, keepdims=True)
                lse_ref[hp * blocks + qb] = top + jnp.log(total)
                p = (p * (1.0 / total)).astype(BF16)
                c = own_heads(nn(v2t[:, :nk], p))
                ctx_t_ref[block(hp, 128), qb * 128 : nk] = c.astype(BF16)
                ctx_ref[qb * 128 : nk, block(hp, 128)] = c.T.astype(BF16)

        waits[1]()

        @pl.loop(0, width // 256)
        def _(i):
            cols = block(i, 256)
            out_ref[:, cols] = (
                h_ref[:, cols].astype(F32) + nn(ctx_ref[...], wo_ref[:, cols]) + ob_ref[:, cols]
            )

    return call(
        body, place, [hidden, gain, shift, qkv_bias, out_bias, group_col, group_row],
        [weights[0] + ((width, qkv_width),), weights[1] + ((width, width),)], after,
        [((length, qkv_width), BF16), ((width, length), BF16),
         ((pairs * blocks, 1, 256), F32), ((length, width), F32)],
        [pltpu.VMEM((length, width), BF16), pltpu.VMEM((blocks, length, 256), F32),
         pltpu.VMEM((length, width), BF16)],
        17,
    )


def mlp_forward(place, weights, after, mid, gain, shift, fc_bias, proj_bias, out_dtype):
    length, width = mid.shape
    wide = fc_bias.shape[1]
    step = 256

    def body(place_ref, h_ref, g_ref, b_ref, fb_ref, pb_ref,
             act_ref, slope_ref, out_ref, fc_ref, proj_ref, a_ref, acc_ref, waits):
        xhat, _ = norm_parts(h_ref[...])
        a_ref[...] = (xhat * g_ref[...] + b_ref[...]).astype(BF16)
        acc_ref[...] = h_ref[...] + pb_ref[...]
        waits[0]()
        waits[1]()

        @pl.loop(0, wide // step)
        def _(i):
            cols = block(i, step)
            f = nn(a_ref[...], fc_ref[:, cols]) + fb_ref[:, cols]
            square = f * f
            c = 0.7978845608028654
            t = jnp.tanh(f * (c + (c * 0.044715) * square))
            half = 0.5 + 0.5 * t
            act = (f * half).astype(BF16)
            act_ref[:, cols] = act
            slope = half + 0.5 * f * (1.0 - t * t) * (c + (3 * c * 0.044715) * square)
            slope_ref[:, cols] = slope.astype(BF16)
            acc_ref[...] += nn(act, proj_ref[cols, :])

        out_ref[...] = acc_ref[...].astype(out_dtype)

    return call(
        body, place, [mid, gain, shift, fc_bias, proj_bias],
        [weights[0] + ((width, wide),), weights[1] + ((wide, width),)], after,
        [((length, wide), BF16), ((length, wide), BF16), ((length, width), out_dtype)],
        [pltpu.VMEM((length, width), BF16), pltpu.VMEM((length, width), F32)],
        19,
    )


def order(nf):
    return [r for r in range(nf) if r & 1], [r for r in range(nf) if not r & 1]


def proj_backward(place, weights, after, upstream, act, slope, nf):
    length, width = upstream.shape
    wide = act.shape[1]
    rows = wide // nf
    away, stay = order(nf)
    step = 256

    def body(place_ref, d_ref, act_ref, slope_ref,
             send_ref, keep_ref, df_ref, fb_ref, pb_ref, proj_ref, dm_ref, waits):
        dm_ref[...] = d_ref[...].astype(BF16)
        pb_ref[...] = jnp.sum(dm_ref[...].astype(F32), axis=0, keepdims=True)
        for target, list_r in ((send_ref, away), (keep_ref, stay)):
            for k, r in enumerate(list_r):
                first = (place_ref[0] ^ r) * rows

                @pl.loop(0, rows // step)
                def _(i, target=target, k=k, first=first):
                    part = act_ref[:, pl.ds(pl.multiple_of(first + i * step, step), step)]
                    target[k, block(i, step), :] = nn(flip(part), dm_ref[...]).astype(BF16)

        waits[0]()

        @pl.loop(0, wide // step)
        def _(i):
            cols = block(i, step)
            d = (nt(dm_ref[...], proj_ref[cols, :]) * slope_ref[:, cols].astype(F32)).astype(BF16)
            df_ref[:, cols] = d
            fb_ref[:, cols] = jnp.sum(d.astype(F32), axis=0, keepdims=True)

    half = (nf // 2, rows, width)
    return call(
        body, place, [upstream, act, slope], [weights[1] + ((wide, width),)], after,
        [(half, BF16), (half, BF16), ((length, wide), BF16), ((1, wide), F32), ((1, width), F32)],
        [pltpu.VMEM((length, width), BF16)],
        16,
    )


def norm_backward(d, xhat, rstd, gain):
    dx = d * gain
    inner = jnp.mean(dx * xhat, axis=-1, keepdims=True)
    back = rstd * (dx - jnp.mean(dx, axis=-1, keepdims=True) - xhat * inner)
    return back, jnp.sum(d * xhat, axis=0, keepdims=True), jnp.sum(d, axis=0, keepdims=True)


def fc_backward(place, weights, after, upstream, df, mid, gain, shift, nf):
    length, width = mid.shape
    wide = df.shape[1]
    rows = width // nf
    away, stay = order(nf)
    step = 256

    def body(place_ref, d_ref, df_ref, h_ref, g_ref, b_ref,
             send_ref, keep_ref, out_ref, gg_ref, sg_ref, fc_ref, at_ref, da_ref, waits):
        xhat, rstd = norm_parts(h_ref[...])
        at_ref[...] = (xhat * g_ref[...] + b_ref[...]).T.astype(BF16)
        for target, list_r in ((send_ref, away), (keep_ref, stay)):
            for k, r in enumerate(list_r):
                first = pl.ds(pl.multiple_of((place_ref[0] ^ r) * rows, 32), rows)

                @pl.loop(0, wide // step)
                def _(i, target=target, k=k, first=first):
                    cols = block(i, step)
                    target[k, :, cols] = nn(at_ref[first, :], df_ref[:, cols]).astype(BF16)

        waits[0]()

        @pl.loop(0, width // step)
        def _(i):
            cols = block(i, step)
            da_ref[:, cols] = nt(df_ref[...], fc_ref[cols, :])

        xhat, rstd = norm_parts(h_ref[...])
        back, gg, sg = norm_backward(da_ref[...], xhat, rstd, g_ref[...])
        gg_ref[...] = gg
        sg_ref[...] = sg
        out_ref[...] = d_ref[...].astype(F32) + back

    half = (nf // 2, rows, wide)
    return call(
        body, place, [upstream, df, mid, gain, shift], [weights[0] + ((width, wide),)], after,
        [(half, BF16), (half, BF16), ((length, width), F32), ((1, width), F32), ((1, width), F32)],
        [pltpu.VMEM((width, length), BF16), pltpu.VMEM((length, width), F32)],
        18,
    )


def attn_backward(
    place, weights, after, upstream, qkv, ctx_t, lse, hidden, gain, shift, group_col, group_row, nf
):
    length, width = hidden.shape
    qkv_width = qkv.shape[1]
    rows = width // nf
    away, stay = order(nf)
    pairs = width // 128
    blocks = length // 128
    step = 256

    def body(place_ref, d_ref, qkv_ref, ct_ref, lse_ref, h_ref, g_ref, b_ref, gc_ref, gr_ref,
             send_ref, keep_ref, out_ref, ob_ref, qvb_ref, gg_ref, sg_ref, wq_ref, wo_ref,
             da_ref, dctx_ref, bias_ref, dqkv_ref, at_ref, dn_ref, dk_ref, dv_ref, waits):
        da_ref[...] = d_ref[...].astype(BF16)
        ob_ref[...] = jnp.sum(da_ref[...].astype(F32), axis=0, keepdims=True)
        xhat, rstd = norm_parts(h_ref[...].astype(F32))
        at_ref[...] = (xhat * g_ref[...] + b_ref[...]).T.astype(BF16)
        fill_bias(bias_ref, gc_ref, gr_ref, place_ref[2])
        waits[1]()

        @pl.loop(0, width // step)
        def _(i):
            cols = block(i, step)
            dctx_ref[:, cols] = nt(da_ref[...], wo_ref[cols, :]).astype(BF16)

        @pl.loop(0, pairs)
        def _(hp):
            q2 = qkv_ref[:, block(hp, 128)] * jnp.asarray(0.125, BF16)
            k2 = qkv_ref[:, block(hp + pairs, 128)]
            v2 = qkv_ref[:, block(hp + 2 * pairs, 128)]
            g2 = dctx_ref[:, block(hp, 128)]
            k2t = flip(k2)
            for qb in reversed(range(blocks)):
                nk = (qb + 1) * 128
                qm = two_heads(q2[qb * 128 : nk])
                gm = two_heads(g2[qb * 128 : nk])
                p = jnp.exp(nt(k2[:nk], qm) + bias_ref[qb, 0:nk, :] - lse_ref[hp * blocks + qb])
                dp = nt(v2[:nk], gm)
                inner = jnp.sum(dp * p, axis=0, keepdims=True)
                ds = (p * (dp - inner)).astype(BF16)
                dv = nn(p.astype(BF16), gm)
                dk = nn(ds, qm)
                if qb == blocks - 1:
                    dv_ref[...] = dv
                    dk_ref[...] = dk
                else:
                    dv_ref[0:nk, :] += dv
                    dk_ref[0:nk, :] += dk
                dq = own_heads(nn(k2t[:, :nk], ds))
                dqkv_ref[qb * 128 : nk, block(hp, 128)] = (dq.T * 0.125).astype(BF16)
            dqkv_ref[:, block(hp + pairs, 128)] = dk_ref[...].astype(BF16)
            dqkv_ref[:, block(hp + 2 * pairs, 128)] = dv_ref[...].astype(BF16)

        for target, list_r in ((send_ref, away), (keep_ref, stay)):
            for k, r in enumerate(list_r):
                first = pl.ds(pl.multiple_of((place_ref[0] ^ r) * rows, 32), rows)

                @pl.loop(0, qkv_width // step)
                def _(i, target=target, k=k, first=first):
                    cols = block(i, step)
                    target[k, :, cols] = nn(at_ref[first, :], dqkv_ref[:, cols]).astype(BF16)

                @pl.loop(0, width // step)
                def _(i, target=target, k=k, first=first):
                    cols = block(i, step)
                    ocols = pl.ds(pl.multiple_of(i * step + qkv_width, step), step)
                    target[k, :, ocols] = nn(ct_ref[first, :], da_ref[:, cols]).astype(BF16)

        waits[0]()

        @pl.loop(0, width // step)
        def _(i):
            cols = block(i, step)
            dn_ref[:, cols] = nt(dqkv_ref[...], wq_ref[cols, :])

        qvb_ref[...] = jnp.sum(dqkv_ref[...].astype(F32), axis=0, keepdims=True)
        xhat, rstd = norm_parts(h_ref[...].astype(F32))
        back, gg, sg = norm_backward(dn_ref[...], xhat, rstd, g_ref[...])
        gg_ref[...] = gg
        sg_ref[...] = sg
        out_ref[...] = d_ref[...] + back

    half = (nf // 2, rows, qkv_width + width)
    return call(
        body, place, [upstream, qkv, ctx_t, lse, hidden, gain, shift, group_col, group_row],
        [weights[0] + ((width, qkv_width),), weights[1] + ((width, width),)], after,
        [(half, BF16), (half, BF16), ((length, width), F32), ((1, width), F32),
         ((1, qkv_width), F32), ((1, width), F32), ((1, width), F32)],
        [pltpu.VMEM((length, width), BF16), pltpu.VMEM((length, width), BF16),
         pltpu.VMEM((blocks, length, 256), F32), pltpu.VMEM((length, qkv_width), BF16),
         pltpu.VMEM((width, length), BF16), pltpu.VMEM((length, width), F32),
         pltpu.VMEM((length, 128), F32), pltpu.VMEM((length, 128), F32)],
        28,
    )


class Reducer:
    def __init__(self, sent, kept, nf, nd):
        self.stages = self.run(sent, kept, nf, nd)
        self.value = None
        self.step()

    def step(self):
        try:
            self.sent, self.got = next(self.stages)
        except StopIteration:
            self.sent = self.got = None
        return self.sent

    def run(self, sent, kept, nf, nd):
        self.got = swap(sent, "fsdp", 0, nf)
        yield sent, self.got
        for bit in range(1, bits_of(nf)):
            got = self.got
            away, stay = order(kept.shape[0])
            pick = lambda v, side: jnp.stack([v[r] for r in side])
            sent = add(pick(kept, away), pick(got, away))
            kept = add(pick(kept, stay), pick(got, stay))
            yield sent, swap(sent, "fsdp", bit, nf)
        kept, got = kept[0], self.got[0]
        pos = lax.axis_index("dp")
        which = pos & 1
        sent = add(take_half(kept, 1 - which, 1), take_half(got, 1 - which, 1))
        kept = add(take_half(kept, which, 1), take_half(got, which, 1))
        yield sent, swap(sent, "dp", 0, nd)
        value = add(kept, self.got)
        for bit in range(1, bits_of(nd)):
            yield value, swap(value, "dp", bit, nd)
            value = add(value, self.got)
        yield value, swap(value, "dp", 0, nd)
        self.value = put_halves(value, self.got, which, 1)


def step_all(reducers):
    live = [r for r in reducers if r.got is not None]
    if len(live) > 1:
        held = lax.optimization_barrier(tuple(r.got for r in live))
        for r, got in zip(live, held):
            r.got = got
    for r in live:
        r.step()


def make_local(nf, nd):
    def local(
        inputs, groups, padding, cotangent, attn_gain, attn_shift, qkv_weight, query_bias,
        value_bias, out_weight, out_bias, mlp_gain, mlp_shift, fc_weight, fc_bias,
        proj_weight, proj_bias,
    ):
        depth_count, rows, qkv_width = qkv_weight.shape
        width = out_weight.shape[2]
        blocks = proj_weight.shape[1] // rows
        length = inputs.shape[1]
        assert inputs.shape[0] == 1 and width == HEADS * 64
        me = lax.axis_index("fsdp")

        eight = jnp.stack(
            [attn_gain, attn_shift, query_bias, value_bias, out_bias, mlp_gain, mlp_shift, proj_bias], 1
        )
        flat = jnp.concatenate([eight.reshape(-1), fc_bias.reshape(-1)])
        lanes = -(-flat.size // rows // 128) * 128
        vec = jnp.zeros((rows * lanes,), BF16).at[: flat.size].set(flat).reshape(rows, lanes)

        attn_w, mlp_w = [], []
        for depth in range(depth_count):
            out_w, start = out_weight[depth], 0
            if depth == 0:
                qkv_held = gather_pieces(qkv_weight[depth], nf, nd)
                out_held = gather_pieces(jnp.concatenate([out_w, vec], axis=1), nf, nd)
            else:
                qkv_held = gather_pieces(jnp.concatenate([qkv_weight[depth], out_w], axis=1), nf, nd)
                out_held, start = qkv_held, qkv_width
            attn_w.append([(qkv_held, 0), (out_held, start)])
            fc_held = gather_pieces(fc_weight[depth], nf, nd)
            mlp_w.append([(fc_held, 0), (gather_pieces(proj_weight[depth], nf, nd), 0)])

        where = lax.axis_index("dp") & 1
        by_r = {}
        for r, part, v in attn_w[0][1][0]:
            v = v[:, width:]
            if part is None:
                by_r[r] = v
            elif part == 0:
                by_r[r] = v
            else:
                first, second = by_r[r], v
                by_r[r] = jnp.where(
                    where == 0,
                    jnp.concatenate([first, second], 0),
                    jnp.concatenate([second, first], 0),
                )
        every = jnp.stack([by_r[r] for r in range(nf)]).reshape(nf, rows * lanes)[:, : flat.size]
        every = jnp.take(every, me ^ jnp.arange(nf), axis=0).astype(F32)
        eights = every[:, : eight.size].reshape(nf, depth_count, 8, rows)
        eights = eights.transpose(1, 2, 0, 3).reshape(depth_count, 8, 1, nf * rows)
        fcs = every[:, eight.size :].reshape(nf, depth_count, -1).transpose(1, 0, 2)
        fcs = fcs.reshape(depth_count, 1, -1)

        valid = length - padding[0]
        place = jnp.stack([me, where, valid]).astype(jnp.int32)
        group_row = groups
        group_col = groups.reshape(length, 1)

        hidden = inputs[0]
        saved = []
        for depth in range(depth_count):
            ag, ash, qb, vb, ob, mg, ms, pb = [eights[depth, i] for i in range(8)]
            qkv_bias = jnp.concatenate([qb, jnp.zeros_like(qb), vb], axis=1)
            qkv, ctx_t, lse, mid = attn_forward(
                place, attn_w[depth], [], hidden, ag, ash, qkv_bias, ob, group_col, group_row
            )
            last = depth == depth_count - 1
            act, slope, result = mlp_forward(
                place, mlp_w[depth], [], mid, mg, ms, fcs[depth], pb, BF16 if last else F32
            )
            saved.append((hidden, qkv, ctx_t, lse, mid, act, slope))
            hidden = result

        upstream = cotangent[0]
        outs = [None] * depth_count
        line = []
        smalls = []
        waits = []

        def advance(*new):
            sent = [r.step() for r in line if r.got is not None]
            line.extend(new)
            return [v for v in sent if v is not None]

        for depth in reversed(range(depth_count)):
            ag, ash, qb, vb, ob, mg, ms, pb = [eights[depth, i] for i in range(8)]
            start, qkv, ctx_t, lse, mid, act, slope = saved[depth]
            send, keep, df, fb_g, pb_g = proj_backward(
                place, mlp_w[depth], waits, upstream, act, slope, nf
            )
            proj_r = Reducer(send, keep, nf, nd)
            waits = advance(proj_r)
            send, keep, lower, mg_g, ms_g = fc_backward(
                place, mlp_w[depth], waits, upstream, df, mid, mg, ms, nf
            )
            fc_r = Reducer(send, keep, nf, nd)
            waits = advance(fc_r)
            send, keep, upstream, ob_g, qv_g, ag_g, as_g = attn_backward(
                place, attn_w[depth], waits, lower, qkv, ctx_t, lse, start, ag, ash,
                group_col, group_row, nf
            )
            attn_r = Reducer(send, keep, nf, nd)
            smalls.append(jnp.concatenate(
                [ag_g, as_g, qv_g[:, :width], qv_g[:, 2 * width :], ob_g, mg_g, ms_g, pb_g,
                 fb_g.reshape(-1, width)], axis=0
            ))
            if depth:
                waits = advance(attn_r)
            else:
                line.append(attn_r)
            outs[depth] = (attn_r, fc_r, proj_r)
        small = jnp.stack(smalls[::-1])
        exchanges = [("fsdp", bit, nf) for bit in range(bits_of(nf))]
        exchanges += [("dp", bit, nd) for bit in range(bits_of(nd))]
        while any(r.got is not None for r in line) or exchanges:
            if exchanges:
                axis, bit, count = exchanges.pop(0)
                small = small + swap(small, axis, bit, count)
            step_all(line)

        eight_o = lax.dynamic_slice_in_dim(small[:, :8], me * rows, rows, 2)
        ag, ash, qb, vb, ob, mg, ms, pb = [eight_o[:, i] for i in range(8)]
        fb = small[:, 8:].reshape(depth_count, -1)
        fb = lax.dynamic_slice_in_dim(fb, me * fc_bias.shape[1], fc_bias.shape[1], 1)
        wide_out = lambda values: jnp.stack([v.astype(F32) for v in values])
        return (
            hidden[None], upstream[None], ag, ash, wide_out([o[0].value[:, :qkv_width] for o in outs]), qb, vb,
            wide_out([o[0].value[:, qkv_width:] for o in outs]), ob, mg, ms, wide_out([o[1].value for o in outs]),
            fb, wide_out([o[2].value for o in outs]), pb,
        )

    return local


def solution(mesh):
    return jax.shard_map(
        make_local(mesh.shape["fsdp"], mesh.shape["dp"]),
        mesh=mesh,
        in_specs=(
            P(("dp", "fsdp"), None, None),
            P(("dp", "fsdp"), None),
            P(("dp", "fsdp")),
            P(("dp", "fsdp"), None, None),
            P(None, "fsdp"),
            P(None, "fsdp"),
            P(None, "fsdp", None),
            P(None, "fsdp"),
            P(None, "fsdp"),
            P(None, "fsdp", None),
            P(None, "fsdp"),
            P(None, "fsdp"),
            P(None, "fsdp"),
            P(None, "fsdp", None),
            P(None, "fsdp"),
            P(None, "fsdp", None),
            P(None, "fsdp"),
        ),
        out_specs=(
            P(("dp", "fsdp"), None, None),
            P(("dp", "fsdp"), None, None),
            P(None, "fsdp"),
            P(None, "fsdp"),
            P(None, "fsdp", None),
            P(None, "fsdp"),
            P(None, "fsdp"),
            P(None, "fsdp", None),
            P(None, "fsdp"),
            P(None, "fsdp"),
            P(None, "fsdp"),
            P(None, "fsdp", None),
            P(None, "fsdp"),
            P(None, "fsdp", None),
            P(None, "fsdp"),
        ),
        check_vma=False,
    )
```

```python
import jax
import jax.numpy as jnp
from jax import lax
from jax.experimental import pallas as pl
from jax.experimental.pallas import tpu as pltpu
from jax.sharding import PartitionSpec as P

HEADS = 12
EPS = 1e-05
BIG = -1e30
VMEM_LIMIT = 56 * 1024 * 1024
F32 = jnp.float32
BF16 = jnp.bfloat16
VM = pl.BlockSpec(memory_space=pltpu.VMEM)
HB = pl.BlockSpec(memory_space=pl.ANY)


def swap(value, axis, bit, count):
    return lax.ppermute(value, axis, [(i, i ^ (1 << bit)) for i in range(count)])


def bits_of(count):
    bits = count.bit_length() - 1
    assert 1 << bits == count
    return bits


def take_half(value, which, dim):
    half = value.shape[dim] // 2
    return lax.dynamic_slice_in_dim(value, which * half, half, dim)


def put_halves(mine, other, which, dim):
    half = mine.shape[dim]
    shape = list(mine.shape)
    shape[dim] = 2 * half
    whole = jnp.zeros(shape, mine.dtype)
    whole = lax.dynamic_update_slice_in_dim(whole, mine, which * half, dim)
    return lax.dynamic_update_slice_in_dim(whole, other, (1 - which) * half, dim)


def add(first, second):
    return (first.astype(F32) + second.astype(F32)).astype(BF16)


def gate(values, tokens):
    values, tokens = list(values), list(tokens)
    if not values or not tokens:
        return values
    count = len(values)

    def kernel(*refs):
        pass

    return list(pl.pallas_call(
        kernel,
        out_shape=[jax.ShapeDtypeStruct(v.shape, v.dtype) for v in values],
        in_specs=[HB] * (count + len(tokens)),
        out_specs=[HB] * count,
        input_output_aliases={i: i for i in range(count)},
    )(*values, *tokens))


class Gather:
    def __init__(self, shards, depth, helper, nf, nd, extra=()):
        self.helper, self.nf, self.nd = helper, nf, nd
        self.top = bits_of(nf) - 1
        which = (lax.axis_index("dp") >> helper) & 1
        halves = [take_half(shard[depth], which, 0) for shard in shards] + list(extra)
        half = halves[0] if len(halves) == 1 else jnp.concatenate(halves, axis=1)
        self.first = swap(half, "fsdp", self.top, nf)

    def near(self):
        self.second = swap(self.first, "dp", self.helper, self.nd)

    def far_pieces(self):
        top = 1 << self.top
        held = [(top, (self.helper, 0), self.first), (top, (self.helper, 1), self.second)]
        for bit in range(self.top):
            held += [(r | (1 << bit), part, swap(v, "fsdp", bit, self.nf)) for r, part, v in held]
        return held


def near_pieces(shard, nf):
    held = [(0, shard)]
    for bit in range(bits_of(nf) - 1):
        held += [(r | (1 << bit), swap(v, "fsdp", bit, nf)) for r, v in held]
    return held


def pieces_of(near, far, depth, start):
    return [(r, None, v, depth, 0) for r, v in near] + [(r, part, v, None, start) for r, part, v in far]


def fetch(held, sources, place_ref, target, sem):
    nf = 1 + max(piece[0] for piece in held)
    rows, width = target.shape[0] // nf, target.shape[1]
    copies = []
    for (r, part, _, depth, start), source in zip(held, sources):
        view = source if depth is None else source.at[depth]
        count = view.shape[0]
        offset = 0 if part is None else (place_ref[2 + part[0]] ^ part[1]) * count
        first = pl.multiple_of((place_ref[0] ^ r) * rows + offset, 32)
        copies.append(
            pltpu.make_async_copy(view.at[:, pl.ds(start, width)], target.at[pl.ds(first, count), :], sem)
        )
    return copies


def start_all(copies):
    for copy in copies:
        copy.start()


def wait_all(copies):
    for copy in copies:
        copy.wait()


def nn(a, b):
    return jnp.dot(a, b, preferred_element_type=F32)


def nt(a, b):
    return lax.dot_general(a, b, (((1,), (1,)), ((), ())), preferred_element_type=F32)


def vec_rows(vec_ref, depth):
    rows = vec_ref[...].astype(F32)
    return [rows[8 * depth + i : 8 * depth + i + 1] for i in range(8)]


def norm_parts(h):
    mean = jnp.mean(h, axis=-1, keepdims=True)
    centred = h - mean
    rstd = lax.rsqrt(jnp.mean(centred * centred, axis=-1, keepdims=True) + EPS)
    return centred * rstd, rstd


def flip(value):
    return value.astype(F32).T.astype(BF16)


def block(i, size):
    return pl.ds(pl.multiple_of(i * size, size), size)


def fill_bias(bias_ref, group_col, group_row, valid):
    length = group_col.shape[0]
    for qb in range(length // 128):
        keys = lax.broadcasted_iota(jnp.int32, (length, 128), 0)
        queries = lax.broadcasted_iota(jnp.int32, (length, 128), 1) + qb * 128
        same = group_col[...] == group_row[:, qb * 128 : (qb + 1) * 128]
        ok = (same & (keys <= queries) & (keys < valid)) | (keys == queries)
        tile = jnp.where(ok, 0.0, BIG).astype(F32)
        bias_ref[qb, :, 0:128] = tile
        bias_ref[qb, :, 128:256] = tile


def two_heads(rows):
    lane = lax.broadcasted_iota(jnp.int32, rows.shape, 1)
    zero = jnp.zeros_like(rows)
    return jnp.concatenate([jnp.where(lane < 64, rows, zero), jnp.where(lane < 64, zero, rows)], axis=0)


def own_heads(tile):
    return jnp.concatenate([tile[0:64, 0:128], tile[64:128, 128:256]], axis=0)


def call(body, place, args, weights, after, out_shape, scratch, micros):
    sources = [piece[2] for held, _ in weights for piece in held]
    n_args, n_out, n_w = len(args), len(out_shape), len(weights)

    def kernel(place_ref, *refs):
        ins = refs[:n_args]
        src = refs[n_args : n_args + len(sources)]
        refs = refs[n_args + len(sources) + len(after) :]
        outs, tiles, sems = refs[:n_out], refs[n_out : n_out + n_w], refs[n_out + n_w : n_out + 2 * n_w]
        copies = []
        for (held, _), tile, sem in zip(weights, tiles, sems):
            copies.append(fetch(held, src[: len(held)], place_ref, tile, sem))
            src = src[len(held) :]
            start_all(copies[-1])
        waits = [lambda c=c: wait_all(c) for c in copies]
        body(place_ref, *ins, *outs, *tiles, *refs[n_out + 2 * n_w :], waits)

    return pl.pallas_call(
        kernel,
        grid_spec=pltpu.PrefetchScalarGridSpec(
            num_scalar_prefetch=1,
            grid=(),
            in_specs=[VM] * n_args + [HB] * (len(sources) + len(after)),
            out_specs=[VM] * n_out,
            scratch_shapes=[pltpu.VMEM(shape, BF16) for _, shape in weights]
            + [pltpu.SemaphoreType.DMA] * n_w + scratch,
        ),
        out_shape=[jax.ShapeDtypeStruct(s, d) for s, d in out_shape],
        compiler_params=pltpu.CompilerParams(vmem_limit_bytes=VMEM_LIMIT),
        cost_estimate=pl.CostEstimate(
            flops=int(micros * 1.15e9), bytes_accessed=1 << 20, transcendentals=0
        ),
    )(place, *args, *sources, *after)


def attn_forward(place, weights, after, hidden, vec, depth, group_col, group_row):
    length, width = hidden.shape
    qkv_width = 3 * width
    pairs = width // 128
    blocks = length // 128

    def body(place_ref, h_ref, vec_ref, gc_ref, gr_ref,
             qkv_ref, ctx_t_ref, lse_ref, out_ref, wq_ref, wo_ref, a_ref, bias_ref, ctx_ref, qb_ref, waits):
        ag, ash, qb, vb, ob, _, _, _ = vec_rows(vec_ref, depth)
        xhat, _ = norm_parts(h_ref[...].astype(F32))
        a_ref[...] = (xhat * ag + ash).astype(BF16)
        qb_ref[...] = jnp.concatenate([qb, jnp.zeros_like(qb), vb], axis=1)
        fill_bias(bias_ref, gc_ref, gr_ref, place_ref[1])
        waits[0]()

        @pl.loop(0, qkv_width // 256)
        def _(i):
            cols = block(i, 256)
            qkv_ref[:, cols] = (nn(a_ref[...], wq_ref[:, cols]) + qb_ref[:, cols]).astype(BF16)

        @pl.loop(0, pairs)
        def _(hp):
            q2 = qkv_ref[:, block(hp, 128)] * jnp.asarray(0.125, BF16)
            k2 = qkv_ref[:, block(hp + pairs, 128)]
            v2t = flip(qkv_ref[:, block(hp + 2 * pairs, 128)])
            for qb in range(blocks):
                nk = (qb + 1) * 128
                s = nt(k2[:nk], two_heads(q2[qb * 128 : nk])) + bias_ref[qb, 0:nk, :]
                top = jnp.max(s, axis=0, keepdims=True)
                p = jnp.exp(s - top)
                total = jnp.sum(p, axis=0, keepdims=True)
                lse_ref[hp * blocks + qb] = top + jnp.log(total)
                p = (p * (1.0 / total)).astype(BF16)
                c = own_heads(nn(v2t[:, :nk], p))
                ctx_t_ref[block(hp, 128), qb * 128 : nk] = c.astype(BF16)
                ctx_ref[qb * 128 : nk, block(hp, 128)] = c.T.astype(BF16)

        waits[1]()

        @pl.loop(0, width // 256)
        def _(i):
            cols = block(i, 256)
            out_ref[:, cols] = h_ref[:, cols].astype(F32) + nn(ctx_ref[...], wo_ref[:, cols])

        out_ref[...] += ob

    return call(
        body, place, [hidden, vec, group_col, group_row],
        [(weights[0], (width, qkv_width)), (weights[1], (width, width))], after,
        [((length, qkv_width), BF16), ((width, length), BF16),
         ((pairs * blocks, 1, 256), F32), ((length, width), F32)],
        [pltpu.VMEM((length, width), BF16), pltpu.VMEM((blocks, length, 256), F32),
         pltpu.VMEM((length, width), BF16), pltpu.VMEM((1, qkv_width), F32)],
        25,
    )


def mlp_forward(place, weights, after, mid, vec, fc_bias, depth, out_dtype):
    length, width = mid.shape
    wide = fc_bias.shape[1]
    step = 256

    def body(place_ref, h_ref, vec_ref, fb_ref,
             act_ref, slope_ref, out_ref, fc_ref, proj_ref, a_ref, acc_ref, waits):
        _, _, _, _, _, mg, ms, pb = vec_rows(vec_ref, depth)
        xhat, _ = norm_parts(h_ref[...])
        a_ref[...] = (xhat * mg + ms).astype(BF16)
        acc_ref[...] = h_ref[...] + pb
        waits[0]()
        waits[1]()

        @pl.loop(0, wide // step)
        def _(i):
            cols = block(i, step)
            f = nn(a_ref[...], fc_ref[:, cols]) + fb_ref[:, cols].astype(F32)[depth : depth + 1]
            square = f * f
            c = 0.7978845608028654
            t = jnp.tanh(f * (c + (c * 0.044715) * square))
            half = 0.5 + 0.5 * t
            act = (f * half).astype(BF16)
            act_ref[:, cols] = act
            slope = half + 0.5 * f * (1.0 - t * t) * (c + (3 * c * 0.044715) * square)
            slope_ref[:, cols] = slope.astype(BF16)
            acc_ref[...] += nn(act, proj_ref[cols, :])

        out_ref[...] = acc_ref[...].astype(out_dtype)

    return call(
        body, place, [mid, vec, fc_bias],
        [(weights[0], (width, wide)), (weights[1], (wide, width))], after,
        [((length, wide), BF16), ((length, wide), BF16), ((length, width), out_dtype)],
        [pltpu.VMEM((length, width), BF16), pltpu.VMEM((length, width), F32)],
        25,
    )


def order(nf):
    return [r for r in range(nf) if r & 1], [r for r in range(nf) if not r & 1]


def targets(ends, nf, place_ref):
    if len(ends) == 1:
        return [(ends[0], s, s) for s in range(nf)]
    return [(ref, k, place_ref[0] ^ r) for ref, side in zip(ends, order(nf)) for k, r in enumerate(side)]


def small_rows(width, wide):
    return -(-(8 + wide // width) // 8) * 8


def proj_backward(place, weights, after, upstream, act, slope, nf, whole):
    length, width = upstream.shape
    wide = act.shape[1]
    rows = wide // nf
    step = 256

    def body(place_ref, d_ref, act_ref, slope_ref, *rest):
        *ends, df_ref, small_ref, proj_ref, dm_ref, fb_ref, waits = rest
        dm_ref[...] = d_ref[...].astype(BF16)
        small_ref[...] = jnp.zeros_like(small_ref)
        small_ref[7:8, :] = jnp.sum(dm_ref[...].astype(F32), axis=0, keepdims=True)
        for target, k, shard in targets(ends, nf, place_ref):

            @pl.loop(0, rows // step)
            def _(i, target=target, k=k, first=shard * rows):
                part = act_ref[:, pl.ds(pl.multiple_of(first + i * step, step), step)]
                target[k, block(i, step), :] = nn(flip(part), dm_ref[...]).astype(BF16)

        waits[0]()

        @pl.loop(0, wide // step)
        def _(i):
            cols = block(i, step)
            d = (nt(dm_ref[...], proj_ref[cols, :]) * slope_ref[:, cols].astype(F32)).astype(BF16)
            df_ref[:, cols] = d
            fb_ref[:, cols] = jnp.sum(d.astype(F32), axis=0, keepdims=True)

        for i in range(wide // width):
            small_ref[8 + i : 9 + i, :] = fb_ref[:, i * width : (i + 1) * width]

    ends = [((nf, rows, width), BF16)] if whole else [((nf // 2, rows, width), BF16)] * 2
    return call(
        body, place, [upstream, act, slope], [(weights[1], (wide, width))], after,
        ends + [((length, wide), BF16), ((small_rows(width, wide), width), F32)],
        [pltpu.VMEM((length, width), BF16), pltpu.VMEM((1, wide), F32)],
        25,
    )


def norm_backward(d, xhat, rstd, gain):
    dx = d * gain
    inner = jnp.mean(dx * xhat, axis=-1, keepdims=True)
    back = rstd * (dx - jnp.mean(dx, axis=-1, keepdims=True) - xhat * inner)
    return back, jnp.sum(d * xhat, axis=0, keepdims=True), jnp.sum(d, axis=0, keepdims=True)


def fc_backward(place, weights, after, upstream, df, mid, vec, small, depth, nf, whole):
    length, width = mid.shape
    wide = df.shape[1]
    rows = width // nf
    step = 256

    def body(place_ref, d_ref, df_ref, h_ref, vec_ref, before_ref, *rest):
        *ends, out_ref, small_ref, fc_ref, at_ref, da_ref, waits = rest
        _, _, _, _, _, mg, ms, _ = vec_rows(vec_ref, depth)
        xhat, rstd = norm_parts(h_ref[...])
        at_ref[...] = (xhat * mg + ms).T.astype(BF16)
        for target, k, shard in targets(ends, nf, place_ref):
            first = pl.ds(pl.multiple_of(shard * rows, 32), rows)

            @pl.loop(0, wide // step)
            def _(i, target=target, k=k, first=first):
                cols = block(i, step)
                target[k, :, cols] = nn(at_ref[first, :], df_ref[:, cols]).astype(BF16)

        waits[0]()

        @pl.loop(0, width // step)
        def _(i):
            cols = block(i, step)
            da_ref[:, cols] = nt(df_ref[...], fc_ref[cols, :])

        xhat, rstd = norm_parts(h_ref[...])
        back, gg, sg = norm_backward(da_ref[...], xhat, rstd, mg)
        small_ref[...] = before_ref[...]
        small_ref[5:6, :] = gg
        small_ref[6:7, :] = sg
        out_ref[...] = d_ref[...].astype(F32) + back

    ends = [((nf, rows, wide), BF16)] if whole else [((nf // 2, rows, wide), BF16)] * 2
    return call(
        body, place, [upstream, df, mid, vec, small], [(weights[0], (width, wide))], after,
        ends + [((length, width), F32), (small.shape, F32)],
        [pltpu.VMEM((width, length), BF16), pltpu.VMEM((length, width), F32)],
        25,
    )


def attn_backward(
    place, weights, after, upstream, qkv, ctx_t, lse, hidden, vec, small, done, depth,
    group_col, group_row, nf, parts,
):
    length, width = hidden.shape
    qkv_width = qkv.shape[1]
    rows = width // nf
    away, stay = order(nf)
    pairs = width // 128
    blocks = length // 128
    step = 256

    layers = 1 + (done[0].shape[0] if done else 0)

    def body(place_ref, d_ref, qkv_ref, ct_ref, lse_ref, h_ref, vec_ref, before_ref, *rest):
        (gc_ref, gr_ref, *ends, out_ref, small_ref, wq_ref, wo_ref,
         da_ref, dctx_ref, bias_ref, dqkv_ref, at_ref, dn_ref, dk_ref, dv_ref, waits) = rest[len(done) :]
        ag, ash = vec_rows(vec_ref, depth)[:2]
        small_ref[0] = before_ref[...]
        for ref in rest[: len(done)]:
            small_ref[1:layers] = ref[...]
        da_ref[...] = d_ref[...].astype(BF16)
        small_ref[0, 4:5, :] = jnp.sum(da_ref[...].astype(F32), axis=0, keepdims=True)
        xhat, rstd = norm_parts(h_ref[...].astype(F32))
        at_ref[...] = (xhat * ag + ash).T.astype(BF16)
        fill_bias(bias_ref, gc_ref, gr_ref, place_ref[1])
        waits[1]()

        @pl.loop(0, width // step)
        def _(i):
            cols = block(i, step)
            dctx_ref[:, cols] = nt(da_ref[...], wo_ref[cols, :]).astype(BF16)

        @pl.loop(0, pairs)
        def _(hp):
            q2 = qkv_ref[:, block(hp, 128)] * jnp.asarray(0.125, BF16)
            k2 = qkv_ref[:, block(hp + pairs, 128)]
            v2 = qkv_ref[:, block(hp + 2 * pairs, 128)]
            g2 = dctx_ref[:, block(hp, 128)]
            k2t = flip(k2)
            for qb in reversed(range(blocks)):
                nk = (qb + 1) * 128
                qm = two_heads(q2[qb * 128 : nk])
                gm = two_heads(g2[qb * 128 : nk])
                p = jnp.exp(nt(k2[:nk], qm) + bias_ref[qb, 0:nk, :] - lse_ref[hp * blocks + qb])
                dp = nt(v2[:nk], gm)
                inner = jnp.sum(dp * p, axis=0, keepdims=True)
                ds = (p * (dp - inner)).astype(BF16)
                dv = nn(p.astype(BF16), gm)
                dk = nn(ds, qm)
                if qb == blocks - 1:
                    dv_ref[...] = dv
                    dk_ref[...] = dk
                else:
                    dv_ref[0:nk, :] += dv
                    dk_ref[0:nk, :] += dk
                dq = own_heads(nn(k2t[:, :nk], ds))
                dqkv_ref[qb * 128 : nk, block(hp, 128)] = (dq.T * 0.125).astype(BF16)
            dqkv_ref[:, block(hp + pairs, 128)] = dk_ref[...].astype(BF16)
            dqkv_ref[:, block(hp + 2 * pairs, 128)] = dv_ref[...].astype(BF16)

        both = qkv_width + width
        for part in range(parts):
            low, high = part * both // parts, (part + 1) * both // parts
            for target, list_r in ((ends[2 * part], away), (ends[2 * part + 1], stay)):
                for k, r in enumerate(list_r):
                    first = pl.ds(pl.multiple_of((place_ref[0] ^ r) * rows, 32), rows)

                    @pl.loop(low // step, min(high, qkv_width) // step)
                    def _(i, target=target, k=k, first=first, low=low):
                        cols = block(i, step)
                        ocols = pl.ds(pl.multiple_of(i * step - low, step), step)
                        target[k, :, ocols] = nn(at_ref[first, :], dqkv_ref[:, cols]).astype(BF16)

                    if high > qkv_width:

                        @pl.loop(0, width // step)
                        def _(i, target=target, k=k, first=first, low=low):
                            cols = block(i, step)
                            ocols = pl.ds(pl.multiple_of(i * step + qkv_width - low, step), step)
                            target[k, :, ocols] = nn(ct_ref[first, :], da_ref[:, cols]).astype(BF16)

        waits[0]()

        @pl.loop(0, width // step)
        def _(i):
            cols = block(i, step)
            dn_ref[:, cols] = nt(dqkv_ref[...], wq_ref[cols, :])

        for row, first in ((2, 0), (3, 2 * width)):
            small_ref[0, row : row + 1, :] = jnp.sum(
                dqkv_ref[:, first : first + width].astype(F32), axis=0, keepdims=True
            )
        xhat, rstd = norm_parts(h_ref[...].astype(F32))
        back, gg, sg = norm_backward(dn_ref[...], xhat, rstd, ag)
        small_ref[0, 0:1, :] = gg
        small_ref[0, 1:2, :] = sg
        out_ref[...] = d_ref[...] + back

    half = (nf // 2, rows, (qkv_width + width) // parts)
    return call(
        body, place, [upstream, qkv, ctx_t, lse, hidden, vec, small] + done + [group_col, group_row],
        [(weights[0], (width, qkv_width)), (weights[1], (width, width))], after,
        [(half, BF16)] * (2 * parts) + [((length, width), F32), ((layers,) + small.shape, F32)],
        [pltpu.VMEM((length, width), BF16), pltpu.VMEM((length, width), BF16),
         pltpu.VMEM((blocks, length, 256), F32), pltpu.VMEM((length, qkv_width), BF16),
         pltpu.VMEM((width, length), BF16), pltpu.VMEM((length, width), F32),
         pltpu.VMEM((length, 128), F32), pltpu.VMEM((length, 128), F32)],
        25,
    )


class Reducer:
    def __init__(self, sent, kept, nf, nd):
        self.stages = self.run(sent, kept, nf, nd)
        self.value = None
        self.step()

    def step(self):
        try:
            self.sent, self.got = next(self.stages)
        except StopIteration:
            self.sent = self.got = None
        return self.sent

    def run(self, sent, kept, nf, nd):
        yield sent, swap(sent, "fsdp", 0, nf)
        for bit in range(1, bits_of(nf)):
            got = self.got
            away, stay = order(kept.shape[0])
            pick = lambda v, side: jnp.stack([v[r] for r in side])
            sent = add(pick(kept, away), pick(got, away))
            kept = add(pick(kept, stay), pick(got, stay))
            yield sent, swap(sent, "fsdp", bit, nf)
        kept, got = kept[0], self.got[0]
        pos = lax.axis_index("dp")
        scattered = [(bit, 1 - bit) for bit in range(min(2, bits_of(nd)))]
        for bit, dim in scattered:
            which = (pos >> bit) & 1
            sent = add(take_half(kept, 1 - which, dim), take_half(got, 1 - which, dim))
            kept = add(take_half(kept, which, dim), take_half(got, which, dim))
            yield sent, swap(sent, "dp", bit, nd)
            got = self.got
        value = add(kept, got)
        for bit in range(len(scattered), bits_of(nd)):
            yield value, swap(value, "dp", bit, nd)
            value = add(value, self.got)
        for bit, dim in reversed(scattered):
            yield value, swap(value, "dp", bit, nd)
            value = put_halves(value, self.got, (pos >> bit) & 1, dim)
        self.value = value


class Everywhere(Reducer):
    def __init__(self, value, nf, nd):
        self.stages = self.run(value, nf, nd)
        self.step()

    def run(self, value, nf, nd):
        for axis, count in (("fsdp", nf), ("dp", nd)):
            for bit in range(bits_of(count)):
                yield value, swap(value, axis, bit, count)
                value = value + self.got
        self.value = value


def advance(reducers, tokens):
    live = [r for r in reducers if r.got is not None]
    for r, got in zip(live, gate([r.got for r in live], tokens)):
        r.got = got
    ends = []
    for r in live:
        got = r.got
        sent = r.step()
        ends.append(got if sent is None else sent)
    return ends


STEPS = ((), (0,), (0, 1), (0, 2), (0, 1, 3), (0, 1, 2, 3, 4))
ROUNDS = (
    (5, 6), (0, 1), (2, 3), (4, 6), (1, 2), (3, 5, 6), (2, 1, 4), (3, 5), (2, 4), (3, 5, 6), (2, 4), (3, 5, 6),
    (4, 5), (4, 5), (5,), (5,),
)


def make_local(nf, nd):
    def local(
        inputs, groups, padding, cotangent, attn_gain, attn_shift, qkv_weight, query_bias,
        value_bias, out_weight, out_bias, mlp_gain, mlp_shift, fc_weight, fc_bias,
        proj_weight, proj_bias,
    ):
        depth_count, rows, qkv_width = qkv_weight.shape
        width = out_weight.shape[2]
        length = inputs.shape[1]
        assert inputs.shape[0] == 1 and width == HEADS * 64
        me = lax.axis_index("fsdp")
        pos = lax.axis_index("dp")

        eight = jnp.stack(
            [attn_gain, attn_shift, query_bias, value_bias, out_bias, mlp_gain, mlp_shift, proj_bias], 1
        ).reshape(depth_count * 8, rows)
        flat = jnp.concatenate([eight, fc_bias.reshape(-1, rows)], axis=0)
        lanes = -(-rows // 256) * 256
        rider = jnp.pad(flat, ((0, rows // 2 - flat.shape[0]), (0, lanes - rows)))

        attn_g, mlp_g = [], []
        for depth in range(depth_count):
            pair = [qkv_weight, out_weight]
            attn_g.append([Gather(pair, depth, 0, nf, nd, () if depth else (rider,))])
            mlp_g.append([Gather([v], depth, i, nf, nd) for i, v in enumerate([fc_weight, proj_weight])])
        near = [near_pieces(v, nf) for v in (qkv_weight, out_weight, fc_weight, proj_weight)]
        near_flat = dict(near_pieces(flat, nf))

        place = jnp.stack(
            [me, length - padding[0]] + [(pos >> bit) & 1 for bit in range(bits_of(nd))]
        ).astype(jnp.int32)
        group_row = groups
        group_col = groups.reshape(length, 1)

        hidden = inputs[0]
        saved = []
        attn_w, mlp_w = [], []

        def hold(gathers, token, half):
            for g, v in zip(gathers, gate([getattr(g, half) for g in gathers], [token])):
                setattr(g, half, v)

        for depth in range(depth_count):
            attn, (fc, proj) = attn_g[depth], mlp_g[depth]
            last = depth == depth_count - 1
            waits = []
            if depth == 0:
                for g in attn + [fc, proj]:
                    g.near()
            else:
                hold([fc, proj], hidden, "first")
                fc.near()
                proj.near()
            waits = [fc.first, proj.first]
            pieces = [g.far_pieces() for g in attn]
            if depth == 0:
                for r, part, v in pieces[0]:
                    if part[1] == 0:
                        near_flat[r] = v[: flat.shape[0], qkv_width + width : qkv_width + width + rows]
                parts = [near_flat[r] for r in range(nf)]
                for bit in range(bits_of(nf)):
                    swapped = [parts[r ^ (1 << bit)] for r in range(nf)]
                    parts = [jnp.where((me >> bit) & 1 == 0, p, q) for p, q in zip(parts, swapped)]
                vec = jnp.concatenate(parts, axis=1)
                fcs = vec[depth_count * 8 :].reshape(depth_count, -1, nf, rows)
                fcs = fcs.transpose(0, 2, 1, 3).reshape(depth_count, -1)
            attn_w.append([
                pieces_of(near[0], pieces[0], depth, 0),
                pieces_of(near[1], pieces[-1], depth, 0 if len(pieces) > 1 else qkv_width),
            ])
            qkv, ctx_t, lse, mid = attn_forward(
                place, attn_w[depth], waits, hidden, vec, depth, group_col, group_row
            )
            waits = []
            ahead = [] if last else attn_g[depth + 1]
            hold([fc, proj], mid, "second")
            hold(ahead, mid, "first")
            for g in ahead:
                g.near()
                waits.append(g.first)
            mlp_w.append([
                pieces_of(near[2 + i], g.far_pieces(), depth, 0) for i, g in enumerate((fc, proj))
            ])
            act, slope, result = mlp_forward(
                place, mlp_w[depth], waits, mid, vec, fcs, depth, BF16 if last else F32
            )
            hold(ahead, result, "second")
            saved.append((hidden, qkv, ctx_t, lse, mid, act, slope))
            hidden = result

        upstream = cotangent[0]
        outs = [None] * depth_count
        line = []
        waits = []
        done = []

        def next_blocks(ends, token):
            number = kernels.pop(0)
            ready = STEPS[number] if number < len(STEPS) else range(len(line))
            sent = advance([line[i] for i in ready], [token])
            for i in range(0, len(ends), 2):
                line.append(Reducer(ends[i], ends[i + 1], nf, nd))
            return sent

        kernels = list(range(3 * depth_count))
        for depth in reversed(range(depth_count)):
            start, qkv, ctx_t, lse, mid, act, slope = saved[depth]
            whole = False
            *ends, df, small = proj_backward(
                place, mlp_w[depth], waits, upstream, act, slope, nf, whole
            )
            waits = next_blocks(ends, df)
            *ends, lower, small = fc_backward(
                place, mlp_w[depth], waits, upstream, df, mid, vec, small, depth, nf, whole
            )
            waits = next_blocks(ends, lower)
            parts = 1
            *ends, upstream, small = attn_backward(
                place, attn_w[depth], waits, lower, qkv, ctx_t, lse, start, vec, small, done, depth,
                group_col, group_row, nf, parts,
            )
            done = [small]
            waits = next_blocks(ends, upstream)
            outs[depth] = [line[-parts:], line[-parts - 2], line[-parts - 1]]
        line.append(Everywhere(small, nf, nd))
        rounds = list(ROUNDS)
        while any(r.got is not None for r in line):
            ready = rounds.pop(0) if rounds else range(len(line))
            waits = advance([line[i] for i in ready], waits) or waits
        small = line[-1].value

        proj_out, fc_out, attn_out = [], [], []
        for o in outs:
            attn_out.append(jnp.concatenate([r.value for r in o[0]], axis=1))
            for v, to in zip(o[1:], (proj_out, fc_out)):
                to.append(v.value)
        eight_o = lax.dynamic_slice_in_dim(small[:, :8], me * rows, rows, 2)
        ag, ash, qb, vb, ob, mg, ms, pb = [eight_o[:, i] for i in range(8)]
        fb = small[:, 8 : 8 + fcs.shape[1] // width].reshape(depth_count, -1)
        fb = lax.dynamic_slice_in_dim(fb, me * fc_bias.shape[1], fc_bias.shape[1], 1)
        wide_out = lambda values: jnp.stack([v.astype(F32) for v in values])
        return (
            hidden[None], upstream[None], ag, ash, wide_out([v[:, :qkv_width] for v in attn_out]),
            qb, vb, wide_out([v[:, qkv_width:] for v in attn_out]), ob, mg, ms,
            wide_out(fc_out), fb, wide_out(proj_out), pb,
        )

    return local


def solution(mesh):
    return jax.shard_map(
        make_local(mesh.shape["fsdp"], mesh.shape["dp"]),
        mesh=mesh,
        in_specs=(
            P(("dp", "fsdp"), None, None),
            P(("dp", "fsdp"), None),
            P(("dp", "fsdp")),
            P(("dp", "fsdp"), None, None),
            P(None, "fsdp"),
            P(None, "fsdp"),
            P(None, "fsdp", None),
            P(None, "fsdp"),
            P(None, "fsdp"),
            P(None, "fsdp", None),
            P(None, "fsdp"),
            P(None, "fsdp"),
            P(None, "fsdp"),
            P(None, "fsdp", None),
            P(None, "fsdp"),
            P(None, "fsdp", None),
            P(None, "fsdp"),
        ),
        out_specs=(
            P(("dp", "fsdp"), None, None),
            P(("dp", "fsdp"), None, None),
            P(None, "fsdp"),
            P(None, "fsdp"),
            P(None, "fsdp", None),
            P(None, "fsdp"),
            P(None, "fsdp"),
            P(None, "fsdp", None),
            P(None, "fsdp"),
            P(None, "fsdp"),
            P(None, "fsdp"),
            P(None, "fsdp", None),
            P(None, "fsdp"),
            P(None, "fsdp", None),
            P(None, "fsdp"),
        ),
        check_vma=False,
    )
```

```python
import jax
import jax.numpy as jnp
from jax import lax
from jax.experimental import pallas as pl
from jax.experimental.pallas import tpu as pltpu
from jax.sharding import PartitionSpec as P

HEADS = 12
EPS = 1e-05
BIG = -1e30
VMEM_LIMIT = 56 * 1024 * 1024
F32 = jnp.float32
BF16 = jnp.bfloat16
VM = pl.BlockSpec(memory_space=pltpu.VMEM)
HB = pl.BlockSpec(memory_space=pl.ANY)


def swap(value, axis, bit, count):
    return lax.ppermute(value, axis, [(i, i ^ (1 << bit)) for i in range(count)])


def bits_of(count):
    bits = count.bit_length() - 1
    assert 1 << bits == count
    return bits


def take_half(value, which, dim):
    half = value.shape[dim] // 2
    return lax.dynamic_slice_in_dim(value, which * half, half, dim)


def put_halves(mine, other, which, dim):
    half = mine.shape[dim]
    shape = list(mine.shape)
    shape[dim] = 2 * half
    whole = jnp.zeros(shape, mine.dtype)
    whole = lax.dynamic_update_slice_in_dim(whole, mine, which * half, dim)
    return lax.dynamic_update_slice_in_dim(whole, other, (1 - which) * half, dim)


def add(first, second):
    return (first.astype(F32) + second.astype(F32)).astype(BF16)


def gate(values, tokens):
    values, tokens = list(values), list(tokens)
    if not values or not tokens:
        return values
    count = len(values)

    def kernel(*refs):
        pass

    return list(pl.pallas_call(
        kernel,
        out_shape=[jax.ShapeDtypeStruct(v.shape, v.dtype) for v in values],
        in_specs=[HB] * (count + len(tokens)),
        out_specs=[HB] * count,
        input_output_aliases={i: i for i in range(count)},
    )(*values, *tokens))


class Gather:
    def __init__(self, shards, depth, helper, nf, nd, extra=()):
        self.helper, self.nf, self.nd = helper, nf, nd
        self.top = bits_of(nf) - 1
        which = (lax.axis_index("dp") >> helper) & 1
        halves = [take_half(shard[depth], which, 0) for shard in shards] + list(extra)
        half = halves[0] if len(halves) == 1 else jnp.concatenate(halves, axis=1)
        self.first = swap(half, "fsdp", self.top, nf)

    def near(self):
        self.second = swap(self.first, "dp", self.helper, self.nd)

    def far_pieces(self):
        top = 1 << self.top
        held = [(top, (self.helper, 0), self.first), (top, (self.helper, 1), self.second)]
        for bit in range(self.top):
            held += [(r | (1 << bit), part, swap(v, "fsdp", bit, self.nf)) for r, part, v in held]
        return held


def near_pieces(shard, nf):
    held = [(0, shard)]
    for bit in range(bits_of(nf) - 1):
        held += [(r | (1 << bit), swap(v, "fsdp", bit, nf)) for r, v in held]
    return held


def pieces_of(near, far, depth, start):
    return [(r, None, v, depth, 0) for r, v in near] + [(r, part, v, None, start) for r, part, v in far]


def fetch(held, sources, place_ref, target, sem):
    nf = 1 + max(piece[0] for piece in held)
    rows, width = target.shape[0] // nf, target.shape[1]
    copies = []
    for (r, part, _, depth, start), source in zip(held, sources):
        view = source if depth is None else source.at[depth]
        count = view.shape[0]
        offset = 0 if part is None else (place_ref[2 + part[0]] ^ part[1]) * count
        first = pl.multiple_of((place_ref[0] ^ r) * rows + offset, 32)
        copies.append(
            pltpu.make_async_copy(view.at[:, pl.ds(start, width)], target.at[pl.ds(first, count), :], sem)
        )
    return copies


def start_all(copies):
    for copy in copies:
        copy.start()


def wait_all(copies):
    for copy in copies:
        copy.wait()


def pack_vectors(place, rows, eight, fc_bias):
    depth_count = fc_bias.shape[0]

    def body(place_ref, *refs):
        out_ref = refs[-1]
        parts = [ref[...].astype(F32) for ref in refs[:-1]]
        lines = [parts[i][d : d + 1] for d in range(depth_count) for i in range(8)]
        for d in range(depth_count):
            for q in range(fc_bias.shape[1] // rows):
                lines.append(parts[8][d : d + 1, q * rows : (q + 1) * rows])
        out_ref[...] = jnp.zeros_like(out_ref)
        out_ref[0 : len(lines), 0:rows] = jnp.concatenate(lines, axis=0).astype(BF16)

    shape = (rows // 2, -(-rows // 256) * 256)
    return local_call(body, place, eight + [fc_bias], [(shape, BF16)])[0]


def unpack_vectors(place, near, far, start, rows, depth_count, fc_rows):
    nf = len(near) + len(far)
    blocks = fc_rows // rows
    count = depth_count * (8 + blocks)
    lanes = near[0][1].shape[1]
    held = -(-count // 16) * 16

    def body(place_ref, *refs):
        vec_ref, fc_ref, land_ref, sem = refs[nf:]
        copies = [
            pltpu.make_async_copy(
                refs[len(near) + i].at[pl.ds(0, held), pl.ds(start, lanes)], land_ref.at[i], sem
            )
            for i in range(len(far))
        ]
        start_all(copies)
        wait_all(copies)
        parts = {r: refs[i][0:held, :].astype(F32)[0:count] for i, (r, _) in enumerate(near)}
        parts |= {r: land_ref[i].astype(F32)[0:count] for i, (r, _) in enumerate(far)}
        for s in range(nf):
            own = parts[0]
            for r in range(1, nf):
                own = jnp.where((place_ref[0] ^ s) == r, parts[r], own)
            own = own[:, 0:rows]
            vec_ref[:, s * rows : (s + 1) * rows] = own
            for d in range(depth_count):
                for q in range(blocks):
                    line = depth_count * 8 + d * blocks + q
                    first = (s * blocks + q) * rows
                    fc_ref[d : d + 1, first : first + rows] = own[line : line + 1]

    return local_call(
        body, place, [v for _, v in near + far],
        [((count, nf * rows), F32), ((depth_count, nf * fc_rows), F32)], (),
        [VM] * len(near) + [HB] * len(far), [VM] * 2,
        [pltpu.VMEM((len(far), held, lanes), BF16), pltpu.SemaphoreType.DMA],
    )


def nn(a, b):
    return jnp.dot(a, b, preferred_element_type=F32)


def nt(a, b):
    return lax.dot_general(a, b, (((1,), (1,)), ((), ())), preferred_element_type=F32)


def vec_rows(vec_ref, depth):
    rows = vec_ref[...].astype(F32)
    return [rows[8 * depth + i : 8 * depth + i + 1] for i in range(8)]


def norm_parts(h):
    mean = jnp.mean(h, axis=-1, keepdims=True)
    centred = h - mean
    rstd = lax.rsqrt(jnp.mean(centred * centred, axis=-1, keepdims=True) + EPS)
    return centred * rstd, rstd


def flip(value):
    return value.astype(F32).T.astype(BF16)


def block(i, size):
    return pl.ds(pl.multiple_of(i * size, size), size)


def fill_bias(bias_ref, group_col, group_row, valid):
    length = group_col.shape[0]
    for qb in range(length // 128):
        keys = lax.broadcasted_iota(jnp.int32, (length, 128), 0)
        queries = lax.broadcasted_iota(jnp.int32, (length, 128), 1) + qb * 128
        same = group_col[...] == group_row[:, qb * 128 : (qb + 1) * 128]
        ok = (same & (keys <= queries) & (keys < valid)) | (keys == queries)
        tile = jnp.where(ok, 0.0, BIG).astype(F32)
        bias_ref[qb, :, 0:128] = tile
        bias_ref[qb, :, 128:256] = tile


def two_heads(rows):
    lane = lax.broadcasted_iota(jnp.int32, rows.shape, 1)
    zero = jnp.zeros_like(rows)
    return jnp.concatenate([jnp.where(lane < 64, rows, zero), jnp.where(lane < 64, zero, rows)], axis=0)


def own_heads(tile):
    return jnp.concatenate([tile[0:64, 0:128], tile[64:128, 128:256]], axis=0)


def call(body, place, args, weights, after, out_shape, scratch, micros):
    sources = [piece[2] for held, _ in weights for piece in held]
    n_args, n_out, n_w = len(args), len(out_shape), len(weights)

    def kernel(place_ref, *refs):
        ins = refs[:n_args]
        src = refs[n_args : n_args + len(sources)]
        refs = refs[n_args + len(sources) + len(after) :]
        outs, tiles, sems = refs[:n_out], refs[n_out : n_out + n_w], refs[n_out + n_w : n_out + 2 * n_w]
        copies = []
        for (held, _), tile, sem in zip(weights, tiles, sems):
            copies.append(fetch(held, src[: len(held)], place_ref, tile, sem))
            src = src[len(held) :]
            start_all(copies[-1])
        waits = [lambda c=c: wait_all(c) for c in copies]
        body(place_ref, *ins, *outs, *tiles, *refs[n_out + 2 * n_w :], waits)

    return pl.pallas_call(
        kernel,
        grid_spec=pltpu.PrefetchScalarGridSpec(
            num_scalar_prefetch=1,
            grid=(),
            in_specs=[VM] * n_args + [HB] * (len(sources) + len(after)),
            out_specs=[VM] * n_out,
            scratch_shapes=[pltpu.VMEM(shape, BF16) for _, shape in weights]
            + [pltpu.SemaphoreType.DMA] * n_w + scratch,
        ),
        out_shape=[jax.ShapeDtypeStruct(s, d) for s, d in out_shape],
        compiler_params=pltpu.CompilerParams(vmem_limit_bytes=VMEM_LIMIT),
        cost_estimate=pl.CostEstimate(
            flops=int(micros * 1.15e9), bytes_accessed=1 << 20, transcendentals=0
        ),
    )(place, *args, *sources, *after)


def attn_forward(place, weights, after, hidden, vec, depth, group_col, group_row):
    length, width = hidden.shape
    qkv_width = 3 * width
    pairs = width // 128
    blocks = length // 128

    def body(place_ref, h_ref, vec_ref, gc_ref, gr_ref,
             qkv_ref, ctx_t_ref, lse_ref, out_ref, wq_ref, wo_ref, a_ref, bias_ref, ctx_ref, qb_ref, waits):
        ag, ash, qb, vb, ob, _, _, _ = vec_rows(vec_ref, depth)
        xhat, _ = norm_parts(h_ref[...].astype(F32))
        a_ref[...] = (xhat * ag + ash).astype(BF16)
        qb_ref[...] = jnp.concatenate([qb, jnp.zeros_like(qb), vb], axis=1)
        fill_bias(bias_ref, gc_ref, gr_ref, place_ref[1])
        waits[0]()

        @pl.loop(0, qkv_width // 256, unroll=True)
        def _(i):
            cols = block(i, 256)
            qkv_ref[:, cols] = (nn(a_ref[...], wq_ref[:, cols]) + qb_ref[:, cols]).astype(BF16)

        @pl.loop(0, pairs, unroll=True)
        def _(hp):
            q2 = qkv_ref[:, block(hp, 128)] * jnp.asarray(0.125, BF16)
            k2 = qkv_ref[:, block(hp + pairs, 128)]
            v2t = flip(qkv_ref[:, block(hp + 2 * pairs, 128)])
            for qb in range(blocks):
                nk = (qb + 1) * 128
                s = nt(k2[:nk], two_heads(q2[qb * 128 : nk])) + bias_ref[qb, 0:nk, :]
                top = jnp.max(s, axis=0, keepdims=True)
                p = jnp.exp(s - top)
                total = jnp.sum(p, axis=0, keepdims=True)
                lse_ref[hp * blocks + qb] = top + jnp.log(total)
                p = (p * (1.0 / total)).astype(BF16)
                c = own_heads(nn(v2t[:, :nk], p))
                ctx_t_ref[block(hp, 128), qb * 128 : nk] = c.astype(BF16)
                ctx_ref[qb * 128 : nk, block(hp, 128)] = c.T.astype(BF16)

        waits[1]()

        @pl.loop(0, width // 256, unroll=True)
        def _(i):
            cols = block(i, 256)
            out_ref[:, cols] = h_ref[:, cols].astype(F32) + nn(ctx_ref[...], wo_ref[:, cols])

        out_ref[...] += ob

    return call(
        body, place, [hidden, vec, group_col, group_row],
        [(weights[0], (width, qkv_width)), (weights[1], (width, width))], after,
        [((length, qkv_width), BF16), ((width, length), BF16),
         ((pairs * blocks, 1, 256), F32), ((length, width), F32)],
        [pltpu.VMEM((length, width), BF16), pltpu.VMEM((blocks, length, 256), F32),
         pltpu.VMEM((length, width), BF16), pltpu.VMEM((1, qkv_width), F32)],
        25,
    )


def mlp_forward(place, weights, after, mid, vec, fc_bias, depth, out_dtype):
    length, width = mid.shape
    wide = fc_bias.shape[1]
    step = 256

    def body(place_ref, h_ref, vec_ref, fb_ref,
             act_ref, slope_ref, out_ref, fc_ref, proj_ref, a_ref, acc_ref, waits):
        _, _, _, _, _, mg, ms, pb = vec_rows(vec_ref, depth)
        xhat, _ = norm_parts(h_ref[...])
        a_ref[...] = (xhat * mg + ms).astype(BF16)
        acc_ref[...] = h_ref[...] + pb
        waits[0]()
        waits[1]()

        @pl.loop(0, wide // step, unroll=True)
        def _(i):
            cols = block(i, step)
            f = nn(a_ref[...], fc_ref[:, cols]) + fb_ref[:, cols].astype(F32)[depth : depth + 1]
            square = f * f
            c = 0.7978845608028654
            t = jnp.tanh(f * (c + (c * 0.044715) * square))
            half = 0.5 + 0.5 * t
            act = (f * half).astype(BF16)
            act_ref[:, cols] = act
            slope = half + 0.5 * f * (1.0 - t * t) * (c + (3 * c * 0.044715) * square)
            slope_ref[:, cols] = slope.astype(BF16)
            acc_ref[...] += nn(act, proj_ref[cols, :])

        out_ref[...] = acc_ref[...].astype(out_dtype)

    return call(
        body, place, [mid, vec, fc_bias],
        [(weights[0], (width, wide)), (weights[1], (wide, width))], after,
        [((length, wide), BF16), ((length, wide), BF16), ((length, width), out_dtype)],
        [pltpu.VMEM((length, width), BF16), pltpu.VMEM((length, width), F32)],
        25,
    )


def order(nf):
    return [r for r in range(nf) if r & 1], [r for r in range(nf) if not r & 1]


def targets(ends, nf, place_ref):
    if len(ends) == 1:
        return [(ends[0], s, s) for s in range(nf)]
    return [(ref, k, place_ref[0] ^ r) for ref, side in zip(ends, order(nf)) for k, r in enumerate(side)]


def small_rows(width, wide):
    return -(-(8 + wide // width) // 8) * 8


def proj_backward(place, weights, after, upstream, act, slope, nf, whole):
    length, width = upstream.shape
    wide = act.shape[1]
    rows = wide // nf
    step = 256

    def body(place_ref, d_ref, act_ref, slope_ref, *rest):
        *ends, df_ref, small_ref, proj_ref, dm_ref, fb_ref, waits = rest
        dm_ref[...] = d_ref[...].astype(BF16)
        small_ref[...] = jnp.zeros_like(small_ref)
        small_ref[7:8, :] = jnp.sum(dm_ref[...].astype(F32), axis=0, keepdims=True)
        for target, k, shard in targets(ends, nf, place_ref):

            @pl.loop(0, rows // step, unroll=True)
            def _(i, target=target, k=k, first=shard * rows):
                part = act_ref[:, pl.ds(pl.multiple_of(first + i * step, step), step)]
                target[k, block(i, step), :] = nn(flip(part), dm_ref[...]).astype(BF16)

        waits[0]()

        @pl.loop(0, wide // step, unroll=True)
        def _(i):
            cols = block(i, step)
            d = (nt(dm_ref[...], proj_ref[cols, :]) * slope_ref[:, cols].astype(F32)).astype(BF16)
            df_ref[:, cols] = d
            fb_ref[:, cols] = jnp.sum(d.astype(F32), axis=0, keepdims=True)

        for i in range(wide // width):
            small_ref[8 + i : 9 + i, :] = fb_ref[:, i * width : (i + 1) * width]

    ends = [((nf, rows, width), BF16)] if whole else [((nf // 2, rows, width), BF16)] * 2
    return call(
        body, place, [upstream, act, slope], [(weights[1], (wide, width))], after,
        ends + [((length, wide), BF16), ((small_rows(width, wide), width), F32)],
        [pltpu.VMEM((length, width), BF16), pltpu.VMEM((1, wide), F32)],
        25,
    )


def norm_backward(d, xhat, rstd, gain):
    dx = d * gain
    inner = jnp.mean(dx * xhat, axis=-1, keepdims=True)
    back = rstd * (dx - jnp.mean(dx, axis=-1, keepdims=True) - xhat * inner)
    return back, jnp.sum(d * xhat, axis=0, keepdims=True), jnp.sum(d, axis=0, keepdims=True)


def fc_backward(place, weights, after, upstream, df, mid, vec, small, depth, nf, whole):
    length, width = mid.shape
    wide = df.shape[1]
    rows = width // nf
    step = 256

    def body(place_ref, d_ref, df_ref, h_ref, vec_ref, before_ref, *rest):
        *ends, out_ref, small_ref, fc_ref, at_ref, da_ref, waits = rest
        _, _, _, _, _, mg, ms, _ = vec_rows(vec_ref, depth)
        xhat, rstd = norm_parts(h_ref[...])
        at_ref[...] = (xhat * mg + ms).T.astype(BF16)
        for target, k, shard in targets(ends, nf, place_ref):
            first = pl.ds(pl.multiple_of(shard * rows, 32), rows)

            @pl.loop(0, wide // step, unroll=True)
            def _(i, target=target, k=k, first=first):
                cols = block(i, step)
                target[k, :, cols] = nn(at_ref[first, :], df_ref[:, cols]).astype(BF16)

        waits[0]()

        @pl.loop(0, width // step, unroll=True)
        def _(i):
            cols = block(i, step)
            da_ref[:, cols] = nt(df_ref[...], fc_ref[cols, :])

        xhat, rstd = norm_parts(h_ref[...])
        back, gg, sg = norm_backward(da_ref[...], xhat, rstd, mg)
        small_ref[...] = before_ref[...]
        small_ref[5:6, :] = gg
        small_ref[6:7, :] = sg
        out_ref[...] = d_ref[...].astype(F32) + back

    ends = [((nf, rows, wide), BF16)] if whole else [((nf // 2, rows, wide), BF16)] * 2
    return call(
        body, place, [upstream, df, mid, vec, small], [(weights[0], (width, wide))], after,
        ends + [((length, width), F32), (small.shape, F32)],
        [pltpu.VMEM((width, length), BF16), pltpu.VMEM((length, width), F32)],
        25,
    )


def attn_backward(
    place, weights, after, upstream, qkv, ctx_t, lse, hidden, vec, small, done, depth,
    group_col, group_row, nf, parts,
):
    length, width = hidden.shape
    qkv_width = qkv.shape[1]
    rows = width // nf
    away, stay = order(nf)
    pairs = width // 128
    blocks = length // 128
    step = 256

    layers = 1 + (done[0].shape[0] if done else 0)

    def body(place_ref, d_ref, qkv_ref, ct_ref, lse_ref, h_ref, vec_ref, before_ref, *rest):
        (gc_ref, gr_ref, *ends, out_ref, small_ref, wq_ref, wo_ref,
         da_ref, dctx_ref, bias_ref, dqkv_ref, at_ref, dn_ref, dk_ref, dv_ref, waits) = rest[len(done) :]
        ag, ash = vec_rows(vec_ref, depth)[:2]
        small_ref[0] = before_ref[...]
        for ref in rest[: len(done)]:
            small_ref[1:layers] = ref[...]
        da_ref[...] = d_ref[...].astype(BF16)
        small_ref[0, 4:5, :] = jnp.sum(da_ref[...].astype(F32), axis=0, keepdims=True)
        xhat, rstd = norm_parts(h_ref[...].astype(F32))
        at_ref[...] = (xhat * ag + ash).T.astype(BF16)
        fill_bias(bias_ref, gc_ref, gr_ref, place_ref[1])
        waits[1]()

        @pl.loop(0, width // step, unroll=True)
        def _(i):
            cols = block(i, step)
            dctx_ref[:, cols] = nt(da_ref[...], wo_ref[cols, :]).astype(BF16)

        @pl.loop(0, pairs, unroll=3)
        def _(hp):
            q2 = qkv_ref[:, block(hp, 128)] * jnp.asarray(0.125, BF16)
            k2 = qkv_ref[:, block(hp + pairs, 128)]
            v2 = qkv_ref[:, block(hp + 2 * pairs, 128)]
            g2 = dctx_ref[:, block(hp, 128)]
            k2t = flip(k2)
            for qb in reversed(range(blocks)):
                nk = (qb + 1) * 128
                qm = two_heads(q2[qb * 128 : nk])
                gm = two_heads(g2[qb * 128 : nk])
                p = jnp.exp(nt(k2[:nk], qm) + bias_ref[qb, 0:nk, :] - lse_ref[hp * blocks + qb])
                dp = nt(v2[:nk], gm)
                inner = jnp.sum(dp * p, axis=0, keepdims=True)
                ds = (p * (dp - inner)).astype(BF16)
                dv = nn(p.astype(BF16), gm)
                dk = nn(ds, qm)
                if qb == blocks - 1:
                    dv_ref[...] = dv
                    dk_ref[...] = dk
                else:
                    dv_ref[0:nk, :] += dv
                    dk_ref[0:nk, :] += dk
                dq = own_heads(nn(k2t[:, :nk], ds))
                dqkv_ref[qb * 128 : nk, block(hp, 128)] = (dq.T * 0.125).astype(BF16)
            dqkv_ref[:, block(hp + pairs, 128)] = dk_ref[...].astype(BF16)
            dqkv_ref[:, block(hp + 2 * pairs, 128)] = dv_ref[...].astype(BF16)

        both = qkv_width + width
        for part in range(parts):
            low, high = part * both // parts, (part + 1) * both // parts
            for target, list_r in ((ends[2 * part], away), (ends[2 * part + 1], stay)):
                for k, r in enumerate(list_r):
                    first = pl.ds(pl.multiple_of((place_ref[0] ^ r) * rows, 32), rows)

                    @pl.loop(low // step, min(high, qkv_width) // step, unroll=True)
                    def _(i, target=target, k=k, first=first, low=low):
                        cols = block(i, step)
                        ocols = pl.ds(pl.multiple_of(i * step - low, step), step)
                        target[k, :, ocols] = nn(at_ref[first, :], dqkv_ref[:, cols]).astype(BF16)

                    if high > qkv_width:

                        @pl.loop(0, width // step, unroll=True)
                        def _(i, target=target, k=k, first=first, low=low):
                            cols = block(i, step)
                            ocols = pl.ds(pl.multiple_of(i * step + qkv_width - low, step), step)
                            target[k, :, ocols] = nn(ct_ref[first, :], da_ref[:, cols]).astype(BF16)

        waits[0]()

        @pl.loop(0, width // step, unroll=True)
        def _(i):
            cols = block(i, step)
            dn_ref[:, cols] = nt(dqkv_ref[...], wq_ref[cols, :])

        for row, first in ((2, 0), (3, 2 * width)):
            small_ref[0, row : row + 1, :] = jnp.sum(
                dqkv_ref[:, first : first + width].astype(F32), axis=0, keepdims=True
            )
        xhat, rstd = norm_parts(h_ref[...].astype(F32))
        back, gg, sg = norm_backward(dn_ref[...], xhat, rstd, ag)
        small_ref[0, 0:1, :] = gg
        small_ref[0, 1:2, :] = sg
        out_ref[...] = d_ref[...] + back

    half = (nf // 2, rows, (qkv_width + width) // parts)
    return call(
        body, place, [upstream, qkv, ctx_t, lse, hidden, vec, small] + done + [group_col, group_row],
        [(weights[0], (width, qkv_width)), (weights[1], (width, width))], after,
        [(half, BF16)] * (2 * parts) + [((length, width), F32), ((layers,) + small.shape, F32)],
        [pltpu.VMEM((length, width), BF16), pltpu.VMEM((length, width), BF16),
         pltpu.VMEM((blocks, length, 256), F32), pltpu.VMEM((length, qkv_width), BF16),
         pltpu.VMEM((width, length), BF16), pltpu.VMEM((length, width), F32),
         pltpu.VMEM((length, 128), F32), pltpu.VMEM((length, 128), F32)],
        25,
    )


def local_call(body, place, args, out_shape, grid=(), in_specs=None, out_specs=None, scratch=(), alias=None):
    return pl.pallas_call(
        body,
        grid_spec=pltpu.PrefetchScalarGridSpec(
            num_scalar_prefetch=1, grid=grid,
            in_specs=in_specs or [VM] * len(args), out_specs=out_specs or [VM] * len(out_shape),
            scratch_shapes=list(scratch),
        ),
        out_shape=[jax.ShapeDtypeStruct(shape, dtype) for shape, dtype in out_shape],
        input_output_aliases=alias or {},
        compiler_params=pltpu.CompilerParams(vmem_limit_bytes=VMEM_LIMIT),
    )(place, *args)


class Reducer:
    def __init__(self, sent, kept, nf, nd):
        self.stages = self.run(sent, kept, nf, nd)
        self.value = None
        self.step()

    def step(self):
        try:
            self.sent, self.got = next(self.stages)
        except StopIteration:
            self.sent = self.got = None
        return self.sent

    def run(self, sent, kept, nf, nd):
        yield sent, swap(sent, "fsdp", 0, nf)
        for bit in range(1, bits_of(nf)):
            got = self.got
            away, stay = order(kept.shape[0])
            pick = lambda v, side: jnp.stack([v[r] for r in side])
            sent = add(pick(kept, away), pick(got, away))
            kept = add(pick(kept, stay), pick(got, stay))
            yield sent, swap(sent, "fsdp", bit, nf)
        kept, got = kept[0], self.got[0]
        pos = lax.axis_index("dp")
        scattered = [(bit, 1 - bit) for bit in range(min(2, bits_of(nd)))]
        for bit, dim in scattered:
            which = (pos >> bit) & 1
            sent = add(take_half(kept, 1 - which, dim), take_half(got, 1 - which, dim))
            kept = add(take_half(kept, which, dim), take_half(got, which, dim))
            yield sent, swap(sent, "dp", bit, nd)
            got = self.got
        value = add(kept, got)
        for bit in range(len(scattered), bits_of(nd)):
            yield value, swap(value, "dp", bit, nd)
            value = add(value, self.got)
        for bit, dim in reversed(scattered):
            yield value, swap(value, "dp", bit, nd)
            value = put_halves(value, self.got, (pos >> bit) & 1, dim)
        self.value = value


class Everywhere(Reducer):
    def __init__(self, value, nf, nd):
        self.stages = self.run(value, nf, nd)
        self.step()

    def run(self, value, nf, nd):
        for axis, count in (("fsdp", nf), ("dp", nd)):
            for bit in range(bits_of(count)):
                yield value, swap(value, axis, bit, count)
                value = value + self.got
        self.value = value


def advance(reducers, tokens):
    live = [r for r in reducers if r.got is not None]
    for r, got in zip(live, gate([r.got for r in live], tokens)):
        r.got = got
    ends = []
    for r in live:
        got = r.got
        sent = r.step()
        ends.append(got if sent is None else sent)
    return ends


STEPS = ((), (0,), (1,), (0, 2), (0, 1, 3), (0, 1, 2, 4))
ROUNDS = (
    (3, 5, 6), (0, 1, 2), (0, 2), (1, 3), (2, 4, 1), (3, 0), (4, 3), (5, 2, 4, 6), (3, 4, 1), (5, 4),
    (5, 2, 6), (5, 3), (5, 4, 6), (5,),
)


def make_local(nf, nd):
    def local(
        inputs, groups, padding, cotangent, attn_gain, attn_shift, qkv_weight, query_bias,
        value_bias, out_weight, out_bias, mlp_gain, mlp_shift, fc_weight, fc_bias,
        proj_weight, proj_bias,
    ):
        depth_count, rows, qkv_width = qkv_weight.shape
        width = out_weight.shape[2]
        length = inputs.shape[1]
        assert inputs.shape[0] == 1 and width == HEADS * 64
        me = lax.axis_index("fsdp")
        pos = lax.axis_index("dp")

        place = jnp.stack(
            [me, length - padding[0]] + [(pos >> bit) & 1 for bit in range(bits_of(nd))]
        ).astype(jnp.int32)
        rider = pack_vectors(
            place, rows,
            [attn_gain, attn_shift, query_bias, value_bias, out_bias, mlp_gain, mlp_shift, proj_bias], fc_bias,
        )

        attn_g, mlp_g = [], []
        for depth in range(depth_count):
            pair = [qkv_weight, out_weight]
            attn_g.append([Gather(pair, depth, 0, nf, nd, () if depth else (rider,))])
            mlp_g.append([Gather([v], depth, i, nf, nd) for i, v in enumerate([fc_weight, proj_weight])])
        near = [near_pieces(v, nf) for v in (qkv_weight, out_weight, fc_weight, proj_weight)]
        near_riders = near_pieces(rider, nf)
        group_row = groups
        group_col = groups.reshape(length, 1)

        hidden = inputs[0]
        saved = []
        attn_w, mlp_w = [], []

        def hold(gathers, token, half):
            for g, v in zip(gathers, gate([getattr(g, half) for g in gathers], [token])):
                setattr(g, half, v)

        for depth in range(depth_count):
            attn, (fc, proj) = attn_g[depth], mlp_g[depth]
            last = depth == depth_count - 1
            waits = []
            if depth == 0:
                for g in attn + [fc, proj]:
                    g.near()
            else:
                hold([fc, proj], hidden, "first")
                fc.near()
                proj.near()
            waits = [fc.first, proj.first]
            pieces = [g.far_pieces() for g in attn]
            if depth == 0:
                far_riders = [(r, v) for r, part, v in pieces[0] if part[1] == 0]
                vec, fcs = unpack_vectors(
                    place, near_riders, far_riders, qkv_width + width, rows, depth_count, fc_bias.shape[1]
                )
            attn_w.append([
                pieces_of(near[0], pieces[0], depth, 0),
                pieces_of(near[1], pieces[-1], depth, 0 if len(pieces) > 1 else qkv_width),
            ])
            qkv, ctx_t, lse, mid = attn_forward(
                place, attn_w[depth], waits, hidden, vec, depth, group_col, group_row
            )
            waits = []
            ahead = [] if last else attn_g[depth + 1]
            hold([fc, proj], mid, "second")
            hold(ahead, mid, "first")
            for g in ahead:
                g.near()
                waits.append(g.first)
            mlp_w.append([
                pieces_of(near[2 + i], g.far_pieces(), depth, 0) for i, g in enumerate((fc, proj))
            ])
            act, slope, result = mlp_forward(
                place, mlp_w[depth], waits, mid, vec, fcs, depth, BF16 if last else F32
            )
            hold(ahead, result, "second")
            saved.append((hidden, qkv, ctx_t, lse, mid, act, slope))
            hidden = result

        upstream = cotangent[0]
        outs = [None] * depth_count
        line = []
        waits = []
        done = []

        def next_blocks(ends, token):
            number = kernels.pop(0)
            ready = STEPS[number] if number < len(STEPS) else range(len(line))
            sent = advance([line[i] for i in ready], [token])
            for i in range(0, len(ends), 2):
                line.append(Reducer(ends[i], ends[i + 1], nf, nd))
            return sent

        kernels = list(range(3 * depth_count))
        for depth in reversed(range(depth_count)):
            start, qkv, ctx_t, lse, mid, act, slope = saved[depth]
            whole = False
            *ends, df, small = proj_backward(
                place, mlp_w[depth], waits, upstream, act, slope, nf, whole
            )
            waits = next_blocks(ends, df)
            *ends, lower, small = fc_backward(
                place, mlp_w[depth], waits, upstream, df, mid, vec, small, depth, nf, whole
            )
            waits = next_blocks(ends, lower)
            parts = 1
            *ends, upstream, small = attn_backward(
                place, attn_w[depth], waits, lower, qkv, ctx_t, lse, start, vec, small, done, depth,
                group_col, group_row, nf, parts,
            )
            done = [small]
            waits = next_blocks(ends, upstream)
            outs[depth] = [line[-parts:], line[-parts - 2], line[-parts - 1]]
        line.append(Everywhere(small, nf, nd))
        rounds = list(ROUNDS)
        while any(r.got is not None for r in line):
            ready = rounds.pop(0) if rounds else range(len(line))
            waits = advance([line[i] for i in ready], waits) or waits
        small = line[-1].value

        proj_out, fc_out, attn_out = [], [], []
        for o in outs:
            attn_out.append(jnp.concatenate([r.value for r in o[0]], axis=1))
            for v, to in zip(o[1:], (proj_out, fc_out)):
                to.append(v.value)
        eight_o = lax.dynamic_slice_in_dim(small[:, :8], me * rows, rows, 2)
        ag, ash, qb, vb, ob, mg, ms, pb = [eight_o[:, i] for i in range(8)]
        fb = small[:, 8 : 8 + fcs.shape[1] // width].reshape(depth_count, -1)
        fb = lax.dynamic_slice_in_dim(fb, me * fc_bias.shape[1], fc_bias.shape[1], 1)
        wide_out = lambda values: jnp.stack([v.astype(F32) for v in values])
        return (
            hidden[None], upstream[None], ag, ash, wide_out([v[:, :qkv_width] for v in attn_out]),
            qb, vb, wide_out([v[:, qkv_width:] for v in attn_out]), ob, mg, ms,
            wide_out(fc_out), fb, wide_out(proj_out), pb,
        )

    return local


def solution(mesh):
    return jax.shard_map(
        make_local(mesh.shape["fsdp"], mesh.shape["dp"]),
        mesh=mesh,
        in_specs=(
            P(("dp", "fsdp"), None, None),
            P(("dp", "fsdp"), None),
            P(("dp", "fsdp")),
            P(("dp", "fsdp"), None, None),
            P(None, "fsdp"),
            P(None, "fsdp"),
            P(None, "fsdp", None),
            P(None, "fsdp"),
            P(None, "fsdp"),
            P(None, "fsdp", None),
            P(None, "fsdp"),
            P(None, "fsdp"),
            P(None, "fsdp"),
            P(None, "fsdp", None),
            P(None, "fsdp"),
            P(None, "fsdp", None),
            P(None, "fsdp"),
        ),
        out_specs=(
            P(("dp", "fsdp"), None, None),
            P(("dp", "fsdp"), None, None),
            P(None, "fsdp"),
            P(None, "fsdp"),
            P(None, "fsdp", None),
            P(None, "fsdp"),
            P(None, "fsdp"),
            P(None, "fsdp", None),
            P(None, "fsdp"),
            P(None, "fsdp"),
            P(None, "fsdp"),
            P(None, "fsdp", None),
            P(None, "fsdp"),
            P(None, "fsdp", None),
            P(None, "fsdp"),
        ),
        check_vma=False,
    )
```

```python
import jax
import jax.numpy as jnp
from jax import lax
from jax.experimental import pallas as pl
from jax.experimental.pallas import tpu as pltpu
from jax.sharding import PartitionSpec as P

HEADS = 12
EPS = 1e-05
BIG = -1e30
VMEM_LIMIT = 56 * 1024 * 1024
F32 = jnp.float32
BF16 = jnp.bfloat16
VM = pl.BlockSpec(memory_space=pltpu.VMEM)
HB = pl.BlockSpec(memory_space=pl.ANY)


def swap(value, axis, bit, count):
    return lax.ppermute(value, axis, [(i, i ^ (1 << bit)) for i in range(count)])


def bits_of(count):
    bits = count.bit_length() - 1
    assert 1 << bits == count
    return bits


def take_half(value, which, dim):
    half = value.shape[dim] // 2
    return lax.dynamic_slice_in_dim(value, which * half, half, dim)


def put_halves(mine, other, which, dim):
    half = mine.shape[dim]
    shape = list(mine.shape)
    shape[dim] = 2 * half
    whole = jnp.zeros(shape, mine.dtype)
    whole = lax.dynamic_update_slice_in_dim(whole, mine, which * half, dim)
    return lax.dynamic_update_slice_in_dim(whole, other, (1 - which) * half, dim)


def add(first, second):
    return (first.astype(F32) + second.astype(F32)).astype(BF16)


def gate(values, tokens):
    values, tokens = list(values), list(tokens)
    if not values or not tokens:
        return values
    count = len(values)

    def kernel(*refs):
        pass

    return list(pl.pallas_call(
        kernel,
        out_shape=[jax.ShapeDtypeStruct(v.shape, v.dtype) for v in values],
        in_specs=[HB] * (count + len(tokens)),
        out_specs=[HB] * count,
        input_output_aliases={i: i for i in range(count)},
    )(*values, *tokens))


class Gather:
    def __init__(self, shards, depth, helper, nf, nd, extra=()):
        self.helper, self.nf, self.nd = helper, nf, nd
        self.top = bits_of(nf) - 1
        which = (lax.axis_index("dp") >> helper) & 1
        halves = [take_half(shard[depth], which, 0) for shard in shards] + list(extra)
        half = halves[0] if len(halves) == 1 else jnp.concatenate(halves, axis=1)
        self.first = swap(half, "fsdp", self.top, nf)

    def near(self):
        self.second = swap(self.first, "dp", self.helper, self.nd)

    def far_pieces(self):
        top = 1 << self.top
        held = [(top, (self.helper, 0), self.first), (top, (self.helper, 1), self.second)]
        for bit in range(self.top):
            held += [(r | (1 << bit), part, swap(v, "fsdp", bit, self.nf)) for r, part, v in held]
        return held


def near_pieces(shard, nf):
    held = [(0, shard)]
    for bit in range(bits_of(nf) - 1):
        held += [(r | (1 << bit), swap(v, "fsdp", bit, nf)) for r, v in held]
    return held


def pieces_of(near, far, depth, start):
    return [(r, None, v, depth, 0) for r, v in near] + [(r, part, v, None, start) for r, part, v in far]


def fetch(held, sources, place_ref, target, sem):
    nf = 1 + max(piece[0] for piece in held)
    rows, width = target.shape[0] // nf, target.shape[1]
    copies = []
    for (r, part, _, depth, start), source in zip(held, sources):
        view = source if depth is None else source.at[depth]
        count = view.shape[0]
        offset = 0 if part is None else (place_ref[2 + part[0]] ^ part[1]) * count
        first = pl.multiple_of((place_ref[0] ^ r) * rows + offset, 32)
        copies.append(
            pltpu.make_async_copy(view.at[:, pl.ds(start, width)], target.at[pl.ds(first, count), :], sem)
        )
    return copies


def start_all(copies):
    for copy in copies:
        copy.start()


def wait_all(copies):
    for copy in copies:
        copy.wait()


def pack_vectors(place, rows, eight, fc_bias):
    depth_count = fc_bias.shape[0]

    def body(place_ref, *refs):
        out_ref = refs[-1]
        parts = [ref[...].astype(F32) for ref in refs[:-1]]
        lines = [parts[i][d : d + 1] for d in range(depth_count) for i in range(8)]
        for d in range(depth_count):
            for q in range(fc_bias.shape[1] // rows):
                lines.append(parts[8][d : d + 1, q * rows : (q + 1) * rows])
        out_ref[...] = jnp.zeros_like(out_ref)
        out_ref[0 : len(lines), 0:rows] = jnp.concatenate(lines, axis=0).astype(BF16)

    shape = (rows // 2, -(-rows // 256) * 256)
    return local_call(body, place, eight + [fc_bias], [(shape, BF16)])[0]


def unpack_vectors(place, near, far, start, rows, depth_count, fc_rows):
    nf = len(near) + len(far)
    blocks = fc_rows // rows
    count = depth_count * (8 + blocks)
    lanes = near[0][1].shape[1]
    held = -(-count // 16) * 16

    def body(place_ref, *refs):
        vec_ref, fc_ref, land_ref, sem = refs[nf:]
        copies = [
            pltpu.make_async_copy(
                refs[len(near) + i].at[pl.ds(0, held), pl.ds(start, lanes)], land_ref.at[i], sem
            )
            for i in range(len(far))
        ]
        start_all(copies)
        wait_all(copies)
        parts = {r: refs[i][0:held, :].astype(F32)[0:count] for i, (r, _) in enumerate(near)}
        parts |= {r: land_ref[i].astype(F32)[0:count] for i, (r, _) in enumerate(far)}
        for s in range(nf):
            own = parts[0]
            for r in range(1, nf):
                own = jnp.where((place_ref[0] ^ s) == r, parts[r], own)
            own = own[:, 0:rows]
            vec_ref[:, s * rows : (s + 1) * rows] = own
            for d in range(depth_count):
                for q in range(blocks):
                    line = depth_count * 8 + d * blocks + q
                    first = (s * blocks + q) * rows
                    fc_ref[d : d + 1, first : first + rows] = own[line : line + 1]

    return local_call(
        body, place, [v for _, v in near + far],
        [((count, nf * rows), F32), ((depth_count, nf * fc_rows), F32)], (),
        [VM] * len(near) + [HB] * len(far), [VM] * 2,
        [pltpu.VMEM((len(far), held, lanes), BF16), pltpu.SemaphoreType.DMA],
    )


def nn(a, b):
    return jnp.dot(a, b, preferred_element_type=F32)


def nt(a, b):
    return lax.dot_general(a, b, (((1,), (1,)), ((), ())), preferred_element_type=F32)


def vec_rows(vec_ref, depth):
    rows = vec_ref[...].astype(F32)
    return [rows[8 * depth + i : 8 * depth + i + 1] for i in range(8)]


def norm_parts(h):
    mean = jnp.mean(h, axis=-1, keepdims=True)
    centred = h - mean
    rstd = lax.rsqrt(jnp.mean(centred * centred, axis=-1, keepdims=True) + EPS)
    return centred * rstd, rstd


def flip(value):
    return value.astype(F32).T.astype(BF16)


def block(i, size):
    return pl.ds(pl.multiple_of(i * size, size), size)


def fill_bias(bias_ref, group_col, group_row, valid):
    length = group_col.shape[0]
    for qb in range(length // 128):
        keys = lax.broadcasted_iota(jnp.int32, (length, 128), 0)
        queries = lax.broadcasted_iota(jnp.int32, (length, 128), 1) + qb * 128
        same = group_col[...] == group_row[:, qb * 128 : (qb + 1) * 128]
        ok = (same & (keys <= queries) & (keys < valid)) | (keys == queries)
        tile = jnp.where(ok, 0.0, BIG).astype(F32)
        bias_ref[qb, :, 0:128] = tile
        bias_ref[qb, :, 128:256] = tile


def two_heads(rows):
    lane = lax.broadcasted_iota(jnp.int32, rows.shape, 1)
    zero = jnp.zeros_like(rows)
    return jnp.concatenate([jnp.where(lane < 64, rows, zero), jnp.where(lane < 64, zero, rows)], axis=0)


def own_heads(tile):
    return jnp.concatenate([tile[0:64, 0:128], tile[64:128, 128:256]], axis=0)


def call(body, place, args, weights, after, out_shape, scratch, micros):
    sources = [piece[2] for held, _ in weights for piece in held]
    n_args, n_out, n_w = len(args), len(out_shape), len(weights)

    def kernel(place_ref, *refs):
        ins = refs[:n_args]
        src = refs[n_args : n_args + len(sources)]
        refs = refs[n_args + len(sources) + len(after) :]
        outs, tiles, sems = refs[:n_out], refs[n_out : n_out + n_w], refs[n_out + n_w : n_out + 2 * n_w]
        copies = []
        for (held, _), tile, sem in zip(weights, tiles, sems):
            copies.append(fetch(held, src[: len(held)], place_ref, tile, sem))
            src = src[len(held) :]
            start_all(copies[-1])
        waits = [lambda c=c: wait_all(c) for c in copies]
        body(place_ref, *ins, *outs, *tiles, *refs[n_out + 2 * n_w :], waits)

    return pl.pallas_call(
        kernel,
        grid_spec=pltpu.PrefetchScalarGridSpec(
            num_scalar_prefetch=1,
            grid=(),
            in_specs=[VM] * n_args + [HB] * (len(sources) + len(after)),
            out_specs=[VM] * n_out,
            scratch_shapes=[pltpu.VMEM(shape, BF16) for _, shape in weights]
            + [pltpu.SemaphoreType.DMA] * n_w + scratch,
        ),
        out_shape=[jax.ShapeDtypeStruct(s, d) for s, d in out_shape],
        compiler_params=pltpu.CompilerParams(vmem_limit_bytes=VMEM_LIMIT),
        cost_estimate=pl.CostEstimate(
            flops=int(micros * 1.15e9), bytes_accessed=1 << 20, transcendentals=0
        ),
    )(place, *args, *sources, *after)


def attn_forward(place, weights, after, hidden, vec, depth, group_col, group_row):
    length, width = hidden.shape
    qkv_width = 3 * width
    pairs = width // 128
    blocks = length // 128

    def body(place_ref, h_ref, vec_ref, gc_ref, gr_ref,
             qkv_ref, ctx_t_ref, lse_ref, out_ref, wq_ref, wo_ref, a_ref, bias_ref, ctx_ref, qb_ref, waits):
        ag, ash, qb, vb, ob, _, _, _ = vec_rows(vec_ref, depth)
        xhat, _ = norm_parts(h_ref[...].astype(F32))
        a_ref[...] = (xhat * ag + ash).astype(BF16)
        qb_ref[...] = jnp.concatenate([qb, jnp.zeros_like(qb), vb], axis=1)
        fill_bias(bias_ref, gc_ref, gr_ref, place_ref[1])
        waits[0]()

        @pl.loop(0, qkv_width // 256, unroll=True)
        def _(i):
            cols = block(i, 256)
            qkv_ref[:, cols] = (nn(a_ref[...], wq_ref[:, cols]) + qb_ref[:, cols]).astype(BF16)

        @pl.loop(0, pairs, unroll=True)
        def _(hp):
            q2 = qkv_ref[:, block(hp, 128)] * jnp.asarray(0.125, BF16)
            k2 = qkv_ref[:, block(hp + pairs, 128)]
            v2t = flip(qkv_ref[:, block(hp + 2 * pairs, 128)])
            for qb in range(blocks):
                nk = (qb + 1) * 128
                s = nt(k2[:nk], two_heads(q2[qb * 128 : nk])) + bias_ref[qb, 0:nk, :]
                top = jnp.max(s, axis=0, keepdims=True)
                p = jnp.exp(s - top)
                total = jnp.sum(p, axis=0, keepdims=True)
                lse_ref[hp * blocks + qb] = top + jnp.log(total)
                p = (p * (1.0 / total)).astype(BF16)
                c = own_heads(nn(v2t[:, :nk], p))
                ctx_t_ref[block(hp, 128), qb * 128 : nk] = c.astype(BF16)
                ctx_ref[qb * 128 : nk, block(hp, 128)] = c.T.astype(BF16)

        waits[1]()

        @pl.loop(0, width // 256, unroll=True)
        def _(i):
            cols = block(i, 256)
            out_ref[:, cols] = h_ref[:, cols].astype(F32) + nn(ctx_ref[...], wo_ref[:, cols])

        out_ref[...] += ob

    return call(
        body, place, [hidden, vec, group_col, group_row],
        [(weights[0], (width, qkv_width)), (weights[1], (width, width))], after,
        [((length, qkv_width), BF16), ((width, length), BF16),
         ((pairs * blocks, 1, 256), F32), ((length, width), F32)],
        [pltpu.VMEM((length, width), BF16), pltpu.VMEM((blocks, length, 256), F32),
         pltpu.VMEM((length, width), BF16), pltpu.VMEM((1, qkv_width), F32)],
        25,
    )


def mlp_forward(place, weights, after, mid, vec, fc_bias, depth, out_dtype):
    length, width = mid.shape
    wide = fc_bias.shape[1]
    step = 768

    def body(place_ref, h_ref, vec_ref, fb_ref,
             act_ref, slope_ref, out_ref, fc_ref, proj_ref, a_ref, acc_ref, waits):
        _, _, _, _, _, mg, ms, pb = vec_rows(vec_ref, depth)
        xhat, _ = norm_parts(h_ref[...])
        a_ref[...] = (xhat * mg + ms).astype(BF16)
        acc_ref[...] = h_ref[...] + pb
        waits[0]()
        waits[1]()

        @pl.loop(0, wide // step, unroll=True)
        def _(i):
            cols = block(i, step)
            f = nn(a_ref[...], fc_ref[:, cols]) + fb_ref[:, cols].astype(F32)[depth : depth + 1]
            square = f * f
            c = 0.7978845608028654
            t = jnp.tanh(f * (c + (c * 0.044715) * square))
            half = 0.5 + 0.5 * t
            act = (f * half).astype(BF16)
            act_ref[:, cols] = act
            slope = half + 0.5 * f * (1.0 - t * t) * (c + (3 * c * 0.044715) * square)
            slope_ref[:, cols] = slope.astype(BF16)
            acc_ref[...] += nn(act, proj_ref[cols, :])

        out_ref[...] = acc_ref[...].astype(out_dtype)

    return call(
        body, place, [mid, vec, fc_bias],
        [(weights[0], (width, wide)), (weights[1], (wide, width))], after,
        [((length, wide), BF16), ((length, wide), BF16), ((length, width), out_dtype)],
        [pltpu.VMEM((length, width), BF16), pltpu.VMEM((length, width), F32)],
        25,
    )


def order(nf):
    return [r for r in range(nf) if r & 1], [r for r in range(nf) if not r & 1]


def targets(ends, nf, place_ref):
    if len(ends) == 1:
        return [(ends[0], s, s) for s in range(nf)]
    return [(ref, k, place_ref[0] ^ r) for ref, side in zip(ends, order(nf)) for k, r in enumerate(side)]


def small_rows(width, wide):
    return -(-(8 + wide // width) // 8) * 8


def proj_backward(place, weights, after, upstream, act, slope, nf, whole):
    length, width = upstream.shape
    wide = act.shape[1]
    rows = wide // nf
    step = 256

    def body(place_ref, d_ref, act_ref, slope_ref, *rest):
        *ends, df_ref, small_ref, proj_ref, dm_ref, fb_ref, waits = rest
        dm_ref[...] = d_ref[...].astype(BF16)
        small_ref[...] = jnp.zeros_like(small_ref)
        small_ref[7:8, :] = jnp.sum(dm_ref[...].astype(F32), axis=0, keepdims=True)
        for target, k, shard in targets(ends, nf, place_ref):

            @pl.loop(0, rows // step, unroll=True)
            def _(i, target=target, k=k, first=shard * rows):
                part = act_ref[:, pl.ds(pl.multiple_of(first + i * step, step), step)]
                target[k, block(i, step), :] = nn(flip(part), dm_ref[...]).astype(BF16)

        waits[0]()

        @pl.loop(0, wide // step, unroll=True)
        def _(i):
            cols = block(i, step)
            d = (nt(dm_ref[...], proj_ref[cols, :]) * slope_ref[:, cols].astype(F32)).astype(BF16)
            df_ref[:, cols] = d
            fb_ref[:, cols] = jnp.sum(d.astype(F32), axis=0, keepdims=True)

        for i in range(wide // width):
            small_ref[8 + i : 9 + i, :] = fb_ref[:, i * width : (i + 1) * width]

    ends = [((nf, rows, width), BF16)] if whole else [((nf // 2, rows, width), BF16)] * 2
    return call(
        body, place, [upstream, act, slope], [(weights[1], (wide, width))], after,
        ends + [((length, wide), BF16), ((small_rows(width, wide), width), F32)],
        [pltpu.VMEM((length, width), BF16), pltpu.VMEM((1, wide), F32)],
        25,
    )


def norm_backward(d, xhat, rstd, gain):
    dx = d * gain
    inner = jnp.mean(dx * xhat, axis=-1, keepdims=True)
    back = rstd * (dx - jnp.mean(dx, axis=-1, keepdims=True) - xhat * inner)
    return back, jnp.sum(d * xhat, axis=0, keepdims=True), jnp.sum(d, axis=0, keepdims=True)


def fc_backward(place, weights, after, upstream, df, mid, vec, small, depth, nf, whole):
    length, width = mid.shape
    wide = df.shape[1]
    rows = width // nf
    step = 256

    def body(place_ref, d_ref, df_ref, h_ref, vec_ref, before_ref, *rest):
        *ends, out_ref, small_ref, fc_ref, at_ref, da_ref, waits = rest
        _, _, _, _, _, mg, ms, _ = vec_rows(vec_ref, depth)
        xhat, rstd = norm_parts(h_ref[...])
        at_ref[...] = (xhat * mg + ms).T.astype(BF16)
        for target, k, shard in targets(ends, nf, place_ref):
            first = pl.ds(pl.multiple_of(shard * rows, 32), rows)

            @pl.loop(0, wide // step, unroll=True)
            def _(i, target=target, k=k, first=first):
                cols = block(i, step)
                target[k, :, cols] = nn(at_ref[first, :], df_ref[:, cols]).astype(BF16)

        waits[0]()

        @pl.loop(0, width // step, unroll=True)
        def _(i):
            cols = block(i, step)
            da_ref[:, cols] = nt(df_ref[...], fc_ref[cols, :])

        xhat, rstd = norm_parts(h_ref[...])
        back, gg, sg = norm_backward(da_ref[...], xhat, rstd, mg)
        small_ref[...] = before_ref[...]
        small_ref[5:6, :] = gg
        small_ref[6:7, :] = sg
        out_ref[...] = d_ref[...].astype(F32) + back

    ends = [((nf, rows, wide), BF16)] if whole else [((nf // 2, rows, wide), BF16)] * 2
    return call(
        body, place, [upstream, df, mid, vec, small], [(weights[0], (width, wide))], after,
        ends + [((length, width), F32), (small.shape, F32)],
        [pltpu.VMEM((width, length), BF16), pltpu.VMEM((length, width), F32)],
        25,
    )


def attn_backward(
    place, weights, after, upstream, qkv, ctx_t, lse, hidden, vec, small, done, depth,
    group_col, group_row, nf, parts,
):
    length, width = hidden.shape
    qkv_width = qkv.shape[1]
    rows = width // nf
    away, stay = order(nf)
    pairs = width // 128
    blocks = length // 128
    step = 256

    layers = 1 + (done[0].shape[0] if done else 0)

    def body(place_ref, d_ref, qkv_ref, ct_ref, lse_ref, h_ref, vec_ref, before_ref, *rest):
        (gc_ref, gr_ref, *ends, out_ref, small_ref, wq_ref, wo_ref,
         da_ref, dctx_ref, bias_ref, dqkv_ref, at_ref, dn_ref, dk_ref, dv_ref, waits) = rest[len(done) :]
        ag, ash = vec_rows(vec_ref, depth)[:2]
        small_ref[0] = before_ref[...]
        for ref in rest[: len(done)]:
            small_ref[1:layers] = ref[...]
        da_ref[...] = d_ref[...].astype(BF16)
        small_ref[0, 4:5, :] = jnp.sum(da_ref[...].astype(F32), axis=0, keepdims=True)
        xhat, rstd = norm_parts(h_ref[...].astype(F32))
        at_ref[...] = (xhat * ag + ash).T.astype(BF16)
        fill_bias(bias_ref, gc_ref, gr_ref, place_ref[1])
        waits[1]()

        @pl.loop(0, width // step, unroll=True)
        def _(i):
            cols = block(i, step)
            dctx_ref[:, cols] = nt(da_ref[...], wo_ref[cols, :]).astype(BF16)

        @pl.loop(0, pairs, unroll=3)
        def _(hp):
            q2 = qkv_ref[:, block(hp, 128)] * jnp.asarray(0.125, BF16)
            k2 = qkv_ref[:, block(hp + pairs, 128)]
            v2 = qkv_ref[:, block(hp + 2 * pairs, 128)]
            g2 = dctx_ref[:, block(hp, 128)]
            k2t = flip(k2)
            for qb in reversed(range(blocks)):
                nk = (qb + 1) * 128
                qm = two_heads(q2[qb * 128 : nk])
                gm = two_heads(g2[qb * 128 : nk])
                p = jnp.exp(nt(k2[:nk], qm) + bias_ref[qb, 0:nk, :] - lse_ref[hp * blocks + qb])
                dp = nt(v2[:nk], gm)
                inner = jnp.sum(dp * p, axis=0, keepdims=True)
                ds = (p * (dp - inner)).astype(BF16)
                dv = nn(p.astype(BF16), gm)
                dk = nn(ds, qm)
                if qb == blocks - 1:
                    dv_ref[...] = dv
                    dk_ref[...] = dk
                else:
                    dv_ref[0:nk, :] += dv
                    dk_ref[0:nk, :] += dk
                dq = own_heads(nn(k2t[:, :nk], ds))
                dqkv_ref[qb * 128 : nk, block(hp, 128)] = (dq.T * 0.125).astype(BF16)
            dqkv_ref[:, block(hp + pairs, 128)] = dk_ref[...].astype(BF16)
            dqkv_ref[:, block(hp + 2 * pairs, 128)] = dv_ref[...].astype(BF16)

        both = qkv_width + width
        for part in range(parts):
            low, high = part * both // parts, (part + 1) * both // parts
            for target, list_r in ((ends[2 * part], away), (ends[2 * part + 1], stay)):
                for k, r in enumerate(list_r):
                    first = pl.ds(pl.multiple_of((place_ref[0] ^ r) * rows, 32), rows)

                    @pl.loop(low // step, min(high, qkv_width) // step, unroll=True)
                    def _(i, target=target, k=k, first=first, low=low):
                        cols = block(i, step)
                        ocols = pl.ds(pl.multiple_of(i * step - low, step), step)
                        target[k, :, ocols] = nn(at_ref[first, :], dqkv_ref[:, cols]).astype(BF16)

                    if high > qkv_width:

                        @pl.loop(0, width // step, unroll=True)
                        def _(i, target=target, k=k, first=first, low=low):
                            cols = block(i, step)
                            ocols = pl.ds(pl.multiple_of(i * step + qkv_width - low, step), step)
                            target[k, :, ocols] = nn(ct_ref[first, :], da_ref[:, cols]).astype(BF16)

        waits[0]()

        @pl.loop(0, width // step, unroll=True)
        def _(i):
            cols = block(i, step)
            dn_ref[:, cols] = nt(dqkv_ref[...], wq_ref[cols, :])

        for row, first in ((2, 0), (3, 2 * width)):
            small_ref[0, row : row + 1, :] = jnp.sum(
                dqkv_ref[:, first : first + width].astype(F32), axis=0, keepdims=True
            )
        xhat, rstd = norm_parts(h_ref[...].astype(F32))
        back, gg, sg = norm_backward(dn_ref[...], xhat, rstd, ag)
        small_ref[0, 0:1, :] = gg
        small_ref[0, 1:2, :] = sg
        out_ref[...] = d_ref[...] + back

    half = (nf // 2, rows, (qkv_width + width) // parts)
    return call(
        body, place, [upstream, qkv, ctx_t, lse, hidden, vec, small] + done + [group_col, group_row],
        [(weights[0], (width, qkv_width)), (weights[1], (width, width))], after,
        [(half, BF16)] * (2 * parts) + [((length, width), F32), ((layers,) + small.shape, F32)],
        [pltpu.VMEM((length, width), BF16), pltpu.VMEM((length, width), BF16),
         pltpu.VMEM((blocks, length, 256), F32), pltpu.VMEM((length, qkv_width), BF16),
         pltpu.VMEM((width, length), BF16), pltpu.VMEM((length, width), F32),
         pltpu.VMEM((length, 128), F32), pltpu.VMEM((length, 128), F32)],
        25,
    )


def local_call(body, place, args, out_shape, grid=(), in_specs=None, out_specs=None, scratch=(), alias=None):
    return pl.pallas_call(
        body,
        grid_spec=pltpu.PrefetchScalarGridSpec(
            num_scalar_prefetch=1, grid=grid,
            in_specs=in_specs or [VM] * len(args), out_specs=out_specs or [VM] * len(out_shape),
            scratch_shapes=list(scratch),
        ),
        out_shape=[jax.ShapeDtypeStruct(shape, dtype) for shape, dtype in out_shape],
        input_output_aliases=alias or {},
        compiler_params=pltpu.CompilerParams(vmem_limit_bytes=VMEM_LIMIT),
    )(place, *args)


class Reducer:
    def __init__(self, sent, kept, nf, nd):
        self.stages = self.run(sent, kept, nf, nd)
        self.value = None
        self.step()

    def step(self):
        try:
            self.sent, self.got = next(self.stages)
        except StopIteration:
            self.sent = self.got = None
        return self.sent

    def run(self, sent, kept, nf, nd):
        yield sent, swap(sent, "fsdp", 0, nf)
        for bit in range(1, bits_of(nf)):
            got = self.got
            away, stay = order(kept.shape[0])
            pick = lambda v, side: jnp.stack([v[r] for r in side])
            sent = add(pick(kept, away), pick(got, away))
            kept = add(pick(kept, stay), pick(got, stay))
            yield sent, swap(sent, "fsdp", bit, nf)
        kept, got = kept[0], self.got[0]
        pos = lax.axis_index("dp")
        scattered = [(bit, 1 - bit) for bit in range(min(2, bits_of(nd)))]
        for bit, dim in scattered:
            which = (pos >> bit) & 1
            sent = add(take_half(kept, 1 - which, dim), take_half(got, 1 - which, dim))
            kept = add(take_half(kept, which, dim), take_half(got, which, dim))
            yield sent, swap(sent, "dp", bit, nd)
            got = self.got
        value = add(kept, got)
        for bit in range(len(scattered), bits_of(nd)):
            yield value, swap(value, "dp", bit, nd)
            value = add(value, self.got)
        for bit, dim in reversed(scattered):
            yield value, swap(value, "dp", bit, nd)
            value = put_halves(value, self.got, (pos >> bit) & 1, dim)
        self.value = value


class Everywhere(Reducer):
    def __init__(self, value, nf, nd):
        self.stages = self.run(value, nf, nd)
        self.step()

    def run(self, value, nf, nd):
        for axis, count in (("fsdp", nf), ("dp", nd)):
            for bit in range(bits_of(count)):
                yield value, swap(value, axis, bit, count)
                value = value + self.got
        self.value = value


def advance(reducers, tokens):
    live = [r for r in reducers if r.got is not None]
    for r, got in zip(live, gate([r.got for r in live], tokens)):
        r.got = got
    ends = []
    for r in live:
        got = r.got
        sent = r.step()
        ends.append(got if sent is None else sent)
    return ends


STEPS = ((), (0,), (1,), (0, 2), (0, 1, 3), (0, 1, 2, 4))
ROUNDS = (
    (3, 5, 6), (0, 1, 2), (0, 2), (1, 3), (2, 4, 1), (3, 0), (4, 3), (5, 2, 4, 6), (3, 4, 1), (5, 4),
    (5, 2, 6), (5, 3), (5, 4, 6), (5,),
)


def make_local(nf, nd):
    def local(
        inputs, groups, padding, cotangent, attn_gain, attn_shift, qkv_weight, query_bias,
        value_bias, out_weight, out_bias, mlp_gain, mlp_shift, fc_weight, fc_bias,
        proj_weight, proj_bias,
    ):
        depth_count, rows, qkv_width = qkv_weight.shape
        width = out_weight.shape[2]
        length = inputs.shape[1]
        assert inputs.shape[0] == 1 and width == HEADS * 64
        me = lax.axis_index("fsdp")
        pos = lax.axis_index("dp")

        place = jnp.stack(
            [me, length - padding[0]] + [(pos >> bit) & 1 for bit in range(bits_of(nd))]
        ).astype(jnp.int32)
        rider = pack_vectors(
            place, rows,
            [attn_gain, attn_shift, query_bias, value_bias, out_bias, mlp_gain, mlp_shift, proj_bias], fc_bias,
        )

        attn_g, mlp_g = [], []
        for depth in range(depth_count):
            pair = [qkv_weight, out_weight]
            attn_g.append([Gather(pair, depth, 0, nf, nd, () if depth else (rider,))])
            mlp_g.append([Gather([v], depth, i, nf, nd) for i, v in enumerate([fc_weight, proj_weight])])
        near = [near_pieces(v, nf) for v in (qkv_weight, out_weight, fc_weight, proj_weight)]
        near_riders = near_pieces(rider, nf)
        group_row = groups
        group_col = groups.reshape(length, 1)

        hidden = inputs[0]
        saved = []
        attn_w, mlp_w = [], []

        def hold(gathers, token, half):
            for g, v in zip(gathers, gate([getattr(g, half) for g in gathers], [token])):
                setattr(g, half, v)

        for depth in range(depth_count):
            attn, (fc, proj) = attn_g[depth], mlp_g[depth]
            last = depth == depth_count - 1
            waits = []
            if depth == 0:
                for g in attn + [fc, proj]:
                    g.near()
            else:
                hold([fc, proj], hidden, "first")
                fc.near()
                proj.near()
            waits = [fc.first, proj.first]
            pieces = [g.far_pieces() for g in attn]
            if depth == 0:
                far_riders = [(r, v) for r, part, v in pieces[0] if part[1] == 0]
                vec, fcs = unpack_vectors(
                    place, near_riders, far_riders, qkv_width + width, rows, depth_count, fc_bias.shape[1]
                )
            attn_w.append([
                pieces_of(near[0], pieces[0], depth, 0),
                pieces_of(near[1], pieces[-1], depth, 0 if len(pieces) > 1 else qkv_width),
            ])
            qkv, ctx_t, lse, mid = attn_forward(
                place, attn_w[depth], waits, hidden, vec, depth, group_col, group_row
            )
            waits = []
            ahead = [] if last else attn_g[depth + 1]
            hold([fc, proj], mid, "second")
            hold(ahead, mid, "first")
            for g in ahead:
                g.near()
                waits.append(g.first)
            mlp_w.append([
                pieces_of(near[2 + i], g.far_pieces(), depth, 0) for i, g in enumerate((fc, proj))
            ])
            act, slope, result = mlp_forward(
                place, mlp_w[depth], waits, mid, vec, fcs, depth, BF16 if last else F32
            )
            hold(ahead, result, "second")
            saved.append((hidden, qkv, ctx_t, lse, mid, act, slope))
            hidden = result

        upstream = cotangent[0]
        outs = [None] * depth_count
        line = []
        waits = []
        done = []

        def next_blocks(ends, token):
            number = kernels.pop(0)
            ready = STEPS[number] if number < len(STEPS) else range(len(line))
            sent = advance([line[i] for i in ready], [token])
            for i in range(0, len(ends), 2):
                line.append(Reducer(ends[i], ends[i + 1], nf, nd))
            return sent

        kernels = list(range(3 * depth_count))
        for depth in reversed(range(depth_count)):
            start, qkv, ctx_t, lse, mid, act, slope = saved[depth]
            whole = False
            *ends, df, small = proj_backward(
                place, mlp_w[depth], waits, upstream, act, slope, nf, whole
            )
            waits = next_blocks(ends, df)
            *ends, lower, small = fc_backward(
                place, mlp_w[depth], waits, upstream, df, mid, vec, small, depth, nf, whole
            )
            waits = next_blocks(ends, lower)
            parts = 1
            *ends, upstream, small = attn_backward(
                place, attn_w[depth], waits, lower, qkv, ctx_t, lse, start, vec, small, done, depth,
                group_col, group_row, nf, parts,
            )
            done = [small]
            waits = next_blocks(ends, upstream)
            outs[depth] = [line[-parts:], line[-parts - 2], line[-parts - 1]]
        line.append(Everywhere(small, nf, nd))
        rounds = list(ROUNDS)
        while any(r.got is not None for r in line):
            ready = rounds.pop(0) if rounds else range(len(line))
            waits = advance([line[i] for i in ready], waits) or waits
        small = line[-1].value

        proj_out, fc_out, attn_out = [], [], []
        for o in outs:
            attn_out.append(jnp.concatenate([r.value for r in o[0]], axis=1))
            for v, to in zip(o[1:], (proj_out, fc_out)):
                to.append(v.value)
        eight_o = lax.dynamic_slice_in_dim(small[:, :8], me * rows, rows, 2)
        ag, ash, qb, vb, ob, mg, ms, pb = [eight_o[:, i] for i in range(8)]
        fb = small[:, 8 : 8 + fcs.shape[1] // width].reshape(depth_count, -1)
        fb = lax.dynamic_slice_in_dim(fb, me * fc_bias.shape[1], fc_bias.shape[1], 1)
        wide_out = lambda values: jnp.stack([v.astype(F32) for v in values])
        return (
            hidden[None], upstream[None], ag, ash, wide_out([v[:, :qkv_width] for v in attn_out]),
            qb, vb, wide_out([v[:, qkv_width:] for v in attn_out]), ob, mg, ms,
            wide_out(fc_out), fb, wide_out(proj_out), pb,
        )

    return local


def solution(mesh):
    return jax.shard_map(
        make_local(mesh.shape["fsdp"], mesh.shape["dp"]),
        mesh=mesh,
        in_specs=(
            P(("dp", "fsdp"), None, None),
            P(("dp", "fsdp"), None),
            P(("dp", "fsdp")),
            P(("dp", "fsdp"), None, None),
            P(None, "fsdp"),
            P(None, "fsdp"),
            P(None, "fsdp", None),
            P(None, "fsdp"),
            P(None, "fsdp"),
            P(None, "fsdp", None),
            P(None, "fsdp"),
            P(None, "fsdp"),
            P(None, "fsdp"),
            P(None, "fsdp", None),
            P(None, "fsdp"),
            P(None, "fsdp", None),
            P(None, "fsdp"),
        ),
        out_specs=(
            P(("dp", "fsdp"), None, None),
            P(("dp", "fsdp"), None, None),
            P(None, "fsdp"),
            P(None, "fsdp"),
            P(None, "fsdp", None),
            P(None, "fsdp"),
            P(None, "fsdp"),
            P(None, "fsdp", None),
            P(None, "fsdp"),
            P(None, "fsdp"),
            P(None, "fsdp"),
            P(None, "fsdp", None),
            P(None, "fsdp"),
            P(None, "fsdp", None),
            P(None, "fsdp"),
        ),
        check_vma=False,
    )
```
